256 devices in a mesh: slab: 128 (over z, y, x), chan: 2 (over core).
Axes of the slice: x: 4, y: 4, z: 8, core: 2. Of those that a mesh axis runs over, the one named last changes fastest.
Arguments:
- features: bfloat16 [256, 256, 4, 128], P(None, 'slab', 'chan'), may hold values from -6 to 6
- first_weight: bfloat16 [3, 3, 3, 256, 256], P(None, None, None, 'chan'), may hold values from -0.078125 to 0.078125
- first_bias: float32 [256], P('chan'), may hold values from -3 to 3
- second_weight: bfloat16 [3, 3, 3, 256, 256], P(None, None, None, 'chan'), may hold values from -0.078125 to 0.078125
- second_bias: float32 [256], P('chan'), may hold values from -3 to 3
- cotangent: bfloat16 [256, 256, 4, 128], P('chan', 'slab'), may hold values from -6 to 6
Outputs:
- output: bfloat16 [256, 256, 4, 128], P('chan', 'slab')
- input_grad: bfloat16 [256, 256, 4, 128], P(None, 'slab', 'chan')
- first_weight_grad: float32 [3, 3, 3, 256, 256], P(None, None, None, 'chan')
- first_bias_grad: float32 [256], P('chan')
- second_weight_grad: float32 [3, 3, 3, 256, 256], P(None, None, None, 'chan')
- second_bias_grad: float32 [256], P('chan')
The draws below stay inside these ranges and needn't reach their ends.
All inputs are finite; a program needn't handle non-finite values.
Results may differ from the reference program's by a relative error of at most 0.019.
Values may be sent and summed in bfloat16 or wider, within the bound.
No kernel may reach another device: no remote copies, remote signals or barrier semaphores. Data moves between devices by JAX's collectives and lax.ppermute only.
A program may use at most 128 MiB of HBM per device.

```python
import math
import jax
import jax.numpy as jnp
from jax import lax

C = 256
NY = 128
NX = 256
NZ = 4


def level_of(own_key, shape, cuts, least, largest):
    factor_of = 1.0
    for position, blocks in cuts:
        steps = jax.random.uniform(jax.random.fold_in(jax.random.fold_in(own_key, 6), position), (blocks,), jnp.float32, least / len(cuts), largest / len(cuts))
        factor_of = factor_of * jnp.repeat(jnp.exp(steps), shape[position] // blocks).reshape((-1,) + (1,) * (len(shape) - 1 - position))
    return factor_of


def scatter_about(rng, shape, width, most, split=(), held_as=jnp.bfloat16):
    array = width * jax.random.normal(rng, shape, jnp.float32)
    if split:
        array = array * level_of(rng, shape, split, -0.22, 0.18)
    return jnp.clip(array, -most, most).astype(held_as)


def setup_inputs(seed: int = 0) -> dict:
    key_list = jax.random.split(jax.random.key(seed), 7)
    features = scatter_about(key_list[0], (C, NX, NZ, NY), 1.0, 6.0, ((1, 128), (2, 2)))
    first_weight = scatter_about(key_list[1], (3, 3, 3, C, C), (27 * C) ** -0.5, 0.078125, ((3, 2),))
    first_bias = scatter_about(key_list[2], (C,), 0.5, 3.0, ((0, 2),), jnp.float32)
    second_weight = scatter_about(key_list[3], (3, 3, 3, C, C), (27 * C) ** -0.5, 0.078125, ((3, 2),))
    second_bias = scatter_about(key_list[4], (C,), 0.5, 3.0, ((0, 2),), jnp.float32)
    cotangent = scatter_about(key_list[5], (C, NX, NZ, NY), 1.0, 6.0, ((0, 2), (1, 128)))
    return {"features": features, "first_weight": first_weight, "first_bias": first_bias, "second_weight": second_weight, "second_bias": second_bias, "cotangent": cotangent}


def slope(value):
    sig = jax.nn.sigmoid(value)
    return sig * (1.0 + value * (1.0 - sig))

def windows(field, offset_sign):
    channels, size_x, size_z, size_y = field.shape
    padded = jnp.pad(field, ((0, 0), (1, 1), (1, 1), (1, 1)))
    result = []
    for tap_x in range(3):
        for tap_z in range(3):
            for tap_y in range(3):
                if offset_sign > 0:
                    start_x, start_z, start_y = (tap_x, tap_z, tap_y)
                else:
                    start_x, start_z, start_y = (2 - tap_x, 2 - tap_z, 2 - tap_y)
                window = padded[:, start_x:start_x + size_x, start_z:start_z + size_z, start_y:start_y + size_y]
                result.append(((tap_x, tap_z, tap_y), window.reshape(channels, -1)))
    return result

def conv_taps(field, weight):
    channels, size_x, size_z, size_y = field.shape
    total = jnp.zeros((weight.shape[3], size_x * size_z * size_y), jnp.float32)
    for taps, window in windows(field, 1):
        total = total + jnp.dot(weight[taps], window, preferred_element_type=jnp.float32)
    return total.reshape(-1, size_x, size_z, size_y)

def transpose_taps(grad, weight):
    channels, size_x, size_z, size_y = grad.shape
    total = jnp.zeros((weight.shape[4], size_x * size_z * size_y), jnp.float32)
    for taps, window in windows(grad, -1):
        total = total + jnp.dot(weight[taps].T, window, preferred_element_type=jnp.float32)
    return total.reshape(-1, size_x, size_z, size_y)

def filter_taps(field, grad):
    flat_grad = grad.reshape(grad.shape[0], -1)
    pieces = []
    for taps, window in windows(field, 1):
        pieces.append(jnp.dot(flat_grad, window.T, preferred_element_type=jnp.float32))
    return jnp.stack(pieces).reshape(3, 3, 3, grad.shape[0], field.shape[0])

def reference(features, first_weight, first_bias, second_weight, second_bias, cotangent):
    scale = 1.0 / math.sqrt(NX * NZ * NY)
    first_sum = conv_taps(features, first_weight) + first_bias[:, None, None, None]
    hidden = jax.nn.silu(first_sum).astype(jnp.bfloat16)
    second_sum = conv_taps(hidden, second_weight) + second_bias[:, None, None, None]
    output = jax.nn.silu(second_sum).astype(jnp.bfloat16)
    grad_second = (cotangent.astype(jnp.float32) * slope(second_sum)).astype(jnp.bfloat16)
    second_weight_grad = filter_taps(hidden, grad_second) * scale
    second_bias_grad = lax.optimization_barrier(jnp.sum(grad_second.astype(jnp.float32), axis=(1, 2, 3))) * scale
    grad_hidden = transpose_taps(grad_second, second_weight)
    grad_first = (grad_hidden * slope(first_sum)).astype(jnp.bfloat16)
    first_weight_grad = filter_taps(features, grad_first) * scale
    first_bias_grad = lax.optimization_barrier(jnp.sum(grad_first.astype(jnp.float32), axis=(1, 2, 3))) * scale
    input_grad = transpose_taps(grad_first, first_weight).astype(jnp.bfloat16)
    return (output, input_grad, first_weight_grad, first_bias_grad, second_weight_grad, second_bias_grad)
```

```python
import functools
import math

import jax
import jax.numpy as jnp
from jax import lax
from jax.experimental import pallas as pl
from jax.experimental.pallas import tpu as pltpu
from jax.sharding import PartitionSpec as P

BF = jnp.bfloat16
F32 = jnp.float32
AXES = ("slab", "chan")
CH = 256
HALF = 128
LANES = 128
PLANE = 512
TAPS = 27
X, Y, Z = 4, 4, 8
DEVICES = 2 * X * Y * Z
ROWS = 28 * HALF
PIECE = 112
ORDERS = ((0, 1, 3, 2), (0, 3, 1, 2))
STREAMS = ((True, ORDERS[0]), (True, ORDERS[1]), (False, ORDERS[0]), (False, ORDERS[1]))
VMEM = pl.BlockSpec(memory_space=pltpu.VMEM)
SMEM = pl.BlockSpec(memory_space=pltpu.SMEM)
ANY = pl.BlockSpec(memory_space=pl.ANY)


def call(kernel, out_shape, in_specs, scratch, flops, moved, name):
    return pl.pallas_call(
        kernel,
        out_shape=out_shape,
        in_specs=in_specs,
        out_specs=jax.tree.map(lambda _: VMEM, out_shape),
        scratch_shapes=scratch,
        compiler_params=pltpu.CompilerParams(vmem_limit_bytes=32 * 2**20),
        cost_estimate=pl.CostEstimate(flops=flops, bytes_accessed=moved, transcendentals=0),
        name=name,
    )


def struct(shape, dtype=BF):
    return jax.ShapeDtypeStruct(shape, dtype)


def place(slab):
    return slab % X, (slab // X) % Y, slab // (X * Y)


def slab_of(x, y, z):
    return (z * Y + y) * X + x


def move(value, target):
    pairs = []
    for line in range(DEVICES):
        to = target(line)
        if to is not None:
            pairs.append((line, to))
    return lax.ppermute(value, AXES, pairs)


def to_sibling(value):
    return move(value, lambda line: line ^ 1)


def halos(plane):
    prev = move(plane, lambda line: line + 1 if line + 1 < DEVICES else None)
    following = move(plane, lambda line: line - 1 if line else None)
    return prev, following


def across(value, along_x, mask):
    def target(line):
        x, y, z = place(line // 2)
        x, y = (x ^ mask, y) if along_x else (x, y ^ mask)
        return slab_of(x, y, z) * 2 + line % 2

    return move(value, target)


def along_z(value, step):
    def target(line):
        x, y, z = place(line // 2)
        return slab_of(x, y, (z + step) % Z) * 2 + line % 2

    return move(value, target)


def shifted(plane, tap):
    if tap == 1:
        return plane
    wide = plane.astype(F32)
    lane = lax.broadcasted_iota(jnp.int32, (wide.shape[0], LANES), 1)
    parts = []
    for row in range(PLANE // LANES):
        part = wide[:, row * LANES : (row + 1) * LANES]
        if tap == 0:
            part = jnp.where(lane == 0, 0.0, pltpu.roll(part, 1, 1))
        else:
            part = jnp.where(lane == LANES - 1, 0.0, pltpu.roll(part, LANES - 1, 1))
        parts.append(part.astype(BF))
    return jnp.concatenate(parts, axis=1)


def fill(views, index, plane):
    zero = jnp.zeros((CH, LANES), BF)
    for tap in range(3):
        views[tap, index, :, 0:LANES] = zero
        views[tap, index, :, LANES + PLANE :] = zero
        views[tap, index, :, LANES : LANES + PLANE] = shifted(plane, tap)


def load_weight(core, own, other, full, sems):
    one = pltpu.make_async_copy(own, full.at[:, pl.ds(core * HALF, HALF), :], sems.at[0])
    two = pltpu.make_async_copy(other, full.at[:, pl.ds(HALF - core * HALF, HALF), :], sems.at[1])
    one.start()
    two.start()
    return one, two


def taps():
    return [(x, z, y) for x in range(3) for z in range(3) for y in range(3)]


def forward(full, views):
    total = None
    for x, z, y in taps():
        term = jnp.dot(
            full[x * 9 + z * 3 + y],
            views[y, x, :, z * LANES : z * LANES + PLANE],
            preferred_element_type=F32,
        )
        total = term if total is None else total + term
    return total


def backward(full, views):
    total = None
    for x, z, y in taps():
        term = lax.dot_general(
            full[TAPS - 1 - (x * 9 + z * 3 + y)],
            views[y, x, :, z * LANES : z * LANES + PLANE],
            (((0,), (0,)), ((), ())),
            preferred_element_type=F32,
        )
        total = term if total is None else total + term
    return total


def sigmoid(value):
    return 1.0 / (1.0 + jnp.exp(-value))


def slope(value):
    sig = sigmoid(value)
    return sig * (1.0 + value * (1.0 - sig))


def fill_three(views, prev, own, following):
    for index, plane in enumerate((prev, own, following)):
        fill(views, index, plane[...])


def first_kernel(pos, prev, own, following, w_own, w_other, bias, sums, hidden, views, full, sems):
    copies = load_weight(pos[0], w_own, w_other, full, sems)
    fill_three(views, prev, own, following)
    for copy in copies:
        copy.wait()
    value = forward(full, views) + bias[...]
    sums[...] = value
    hidden[...] = (value * sigmoid(value)).astype(BF)


def second_kernel(
    pos, prev, own, following, w_own, w_other, bias, cot_own, cot_other, output, grad, views, full, cot, sems
):
    core = pos[0]
    copies = load_weight(core, w_own, w_other, full, sems)
    fill_three(views, prev, own, following)
    cot[pl.ds(core * HALF, HALF), :] = cot_own[...]
    cot[pl.ds(HALF - core * HALF, HALF), :] = cot_other[...]
    for copy in copies:
        copy.wait()
    value = forward(full, views) + bias[...]
    output[...] = (value * sigmoid(value)).astype(BF)
    grad[...] = (cot[...].astype(F32) * slope(value)).astype(BF)


def hidden_grad_kernel(pos, prev, own, following, w_own, w_other, sums, grad, views, full, sems):
    copies = load_weight(pos[0], w_own, w_other, full, sems)
    fill_three(views, prev, own, following)
    for copy in copies:
        copy.wait()
    grad[...] = (backward(full, views) * slope(sums[...])).astype(BF)


def input_grad_kernel(pos, prev, own, following, w_own, w_other, grad, views, full, sems):
    copies = load_weight(pos[0], w_own, w_other, full, sems)
    fill_three(views, prev, own, following)
    for copy in copies:
        copy.wait()
    grad[...] = backward(full, views).astype(BF)


CONV_SCRATCH = [
    pltpu.VMEM((3, 3, CH, PLANE + 2 * LANES), BF),
    pltpu.VMEM((TAPS, CH, CH), BF),
]
CONV_FLOPS = 2 * TAPS * CH * CH * PLANE
SEMS = pltpu.SemaphoreType.DMA((2,))


def conv_call(kernel, out_shape, extra, scratch, name):
    return call(
        kernel,
        out_shape,
        [SMEM, VMEM, VMEM, VMEM, ANY, ANY] + [VMEM] * extra,
        CONV_SCRATCH + scratch + [SEMS],
        CONV_FLOPS,
        8 * 2**20,
        name,
    )


def piece_place(pos, stream, outer, inner):
    first_x, order = STREAMS[stream]
    mx, my = (order[outer], order[inner]) if first_x else (order[inner], order[outer])
    return (pos[2] ^ my) * X + (pos[1] ^ mx)


def weight_kernel(pos, prev, own, following, far, grad_own, grad_other, *refs):
    sends, keeps = refs[0:4], refs[4:8]
    views, grads, rows = refs[8:]
    core = pos[0]
    for index, plane in enumerate((prev, own, following)):
        fill(views, core + index, plane[...])
    fill(views, 3 - 3 * core, far[...])
    grads[core] = grad_own[pl.ds(core * HALF, HALF), :]
    grads[1 - core] = grad_other[...]
    one, two = grads[0], grads[1]
    for x, z, y in taps():
        tap = x * 9 + z * 3 + y
        total = None
        for index, grad in enumerate((one, two)):
            term = lax.dot_general(
                grad,
                views[y, x + index, :, z * LANES : z * LANES + PLANE],
                (((1,), (1,)), ((), ())),
                preferred_element_type=F32,
            )
            total = term if total is None else total + term
        total = total.astype(BF)
        rows[tap * HALF : (tap + 1) * HALF, :] = total[:, :HALF]
        rows[ROWS + tap * HALF : ROWS + (tap + 1) * HALF, :] = total[:, HALF:]
    bias = jnp.zeros((HALF, LANES), F32)
    for grad in (one, two):
        for row in range(PLANE // LANES):
            bias = bias + grad[:, row * LANES : (row + 1) * LANES].astype(F32)
    rows[TAPS * HALF : ROWS, :] = bias.astype(BF)
    rows[ROWS + TAPS * HALF :, :] = jnp.zeros((HALF, LANES), BF)
    for stream in range(4):
        for outer in range(4):
            for inner in range(4):
                chunk = piece_place(pos, stream, outer, inner)
                start = pl.multiple_of(chunk * (4 * PIECE) + stream * PIECE, 16)
                target = keeps[stream] if outer < 2 else sends[stream]
                target[(outer % 2) * 4 + inner] = rows[pl.ds(start, PIECE), :]


def weight_terms(pos, planes, far, grad_own, grad_other, name):
    return call(
        weight_kernel,
        [struct((8, PIECE, LANES))] * 8,
        [SMEM] + [VMEM] * 6,
        [
            pltpu.VMEM((3, 4, CH, PLANE + 2 * LANES), BF),
            pltpu.VMEM((2, HALF, PLANE), BF),
            pltpu.VMEM((2 * ROWS, LANES), BF),
        ],
        2 * CONV_FLOPS // 2,
        5 * 2**20,
        name,
    )(pos, *planes, far, grad_own, grad_other)


def added(one, two):
    return (one.astype(F32) + two.astype(F32)).astype(BF)


def merge_kernel(*refs):
    for stream in range(4):
        send, keep = refs[16 + stream], refs[20 + stream]
        for weight in range(2):
            kept, came = refs[weight * 8 + stream], refs[weight * 8 + 4 + stream]
            for slot in range(4):
                keep[slot, weight] = added(kept[slot], came[slot])
                send[slot, weight] = added(kept[4 + slot], came[4 + slot])


def halve_kernel(slots, *refs):
    for stream in range(4):
        kept, came, send, keep = (refs[4 * i + stream] for i in range(4))
        keep[...] = added(kept[0:slots], came[0:slots])
        send[...] = added(kept[slots : 2 * slots], came[slots : 2 * slots])


def spread_kernel(pos, *refs):
    kept, came, pieces, work = refs[0:4], refs[4:8], refs[8:16], refs[16]
    for weight in range(2):
        for stream in range(4):
            work[weight * 4 + stream] = added(kept[stream][0, weight], came[stream][0, weight])
    for step in range(Z):
        pieces[step][...] = work[(pos[3] + step) % Z]


def close_kernel(*refs):
    total = refs[0][...].astype(F32)
    for ref in refs[1:Z]:
        total = total + ref[...].astype(F32)
    refs[Z][...] = total.astype(BF)


def final_kernel(scale, pos, *refs):
    held, came = refs[0:4], refs[4:8]
    first, second, first_bias, second_bias, rows = refs[8:]
    for stream in range(4):
        for outer in range(4):
            for inner in range(4):
                chunk = piece_place(pos, stream, outer, inner)
                source = held[stream] if outer < 2 else came[stream]
                for part in range(2):
                    index = (pos[3] + stream * 2 + part) % Z
                    start = chunk * (4 * PIECE) + (index % 4) * PIECE
                    rows[index // 4, pl.ds(pl.multiple_of(start, 16), PIECE), :] = source[
                        (outer % 2) * 4 + inner, part
                    ]
    for weight, (target, bias) in enumerate(((first, first_bias), (second, second_bias))):
        for tap in range(TAPS):
            for side in range(2):
                start = side * ROWS + tap * HALF
                target[tap, :, side * HALF : (side + 1) * HALF] = (
                    rows[weight, start : start + HALF, :].astype(F32) * scale
                )
        bias[...] = (
            jnp.sum(rows[weight, TAPS * HALF : ROWS, :].astype(F32), axis=1, keepdims=True) * scale
        )


def reduced(pos, first, second, scale):
    came = []
    for terms in (second, first):
        got = []
        for stream, (first_x, order) in enumerate(STREAMS):
            got.append(across(terms[stream], first_x, order[2]))
        came.append(got)
    got2, got1 = came
    merged = call(
        merge_kernel,
        [struct((4, 2, PIECE, LANES))] * 8,
        [VMEM] * 16,
        [],
        2**21,
        6 * 2**20,
        "merge",
    )(*first[4:8], *got1, *second[4:8], *got2)
    send, keep = merged[0:4], merged[4:8]
    for step, slots in ((1, 2), (2, 1)):
        came = []
        for stream, (first_x, order) in enumerate(STREAMS):
            if step == 2:
                first_x = not first_x
            came.append(across(send[stream], first_x, order[1] if step == 1 else order[2]))
        halved = call(
            functools.partial(halve_kernel, slots),
            [struct((slots, 2, PIECE, LANES))] * 8,
            [VMEM] * 8,
            [],
            2**20,
            2 * 2**20,
            f"halve{slots}",
        )(*keep, *came)
        send, keep = halved[0:4], halved[4:8]
    came = []
    for stream, (first_x, order) in enumerate(STREAMS):
        came.append(across(send[stream], not first_x, order[1]))
    pieces = call(
        spread_kernel,
        [struct((PIECE, LANES))] * Z,
        [SMEM] + [VMEM] * 8,
        [pltpu.VMEM((Z, PIECE, LANES), BF)],
        2**19,
        2**20,
        "spread",
    )(pos, *keep, *came)
    came = [along_z(pieces[step], step) for step in range(1, Z)]
    own = call(
        close_kernel,
        struct((PIECE, LANES)),
        [VMEM] * Z,
        [],
        2**18,
        2**18,
        "close",
    )(pieces[0], *came)
    ring = [own] + [along_z(own, -step) for step in range(1, Z)]
    held = [jnp.stack(ring[2 * stream : 2 * stream + 2])[None] for stream in range(4)]
    for step in range(4):
        came = []
        for stream, (first_x, order) in enumerate(STREAMS):
            mask = order[1] if step % 2 == 0 else order[2]
            came.append(across(held[stream], first_x if step >= 2 else not first_x, mask))
        if step < 3:
            held = [jnp.concatenate(pair) for pair in zip(held, came)]
    return call(
        functools.partial(final_kernel, scale),
        [
            struct((TAPS, HALF, CH), F32),
            struct((TAPS, HALF, CH), F32),
            struct((HALF, 1), F32),
            struct((HALF, 1), F32),
        ],
        [SMEM] + [VMEM] * 8,
        [pltpu.VMEM((2, 2 * ROWS, LANES), BF)],
        2**22,
        12 * 2**20,
        "final",
    )(pos, *held, *came)


def per_device(features, first_weight, first_bias, second_weight, second_bias, cotangent):
    core = lax.axis_index("chan")
    even = core == 0
    x, y, z = place(lax.axis_index("slab"))
    pos = jnp.stack([core, x, y, z]).astype(jnp.int32)
    first_weight = first_weight.reshape(TAPS, HALF, CH)
    second_weight = second_weight.reshape(TAPS, HALF, CH)

    split = features.reshape(CH, 2, 2 * LANES)
    kept = jnp.where(even, split[:, 0], split[:, 1])
    came = to_sibling(jnp.where(even, split[:, 1], split[:, 0]))
    plane = jnp.where(
        even, jnp.concatenate([kept, came], axis=1), jnp.concatenate([came, kept], axis=1)
    )
    biases = jnp.stack([first_bias, second_bias])
    other_biases = to_sibling(biases)
    biases = jnp.where(
        even,
        jnp.concatenate([biases, other_biases], axis=1),
        jnp.concatenate([other_biases, biases], axis=1),
    )
    first_other = to_sibling(first_weight)
    prev, following = halos(plane)
    features_near = (prev, plane, following)

    first_sum, hidden = conv_call(
        first_kernel, [struct((CH, PLANE), F32), struct((CH, PLANE))], 1, [], "first"
    )(pos, *features_near, first_weight, first_other, biases[0][:, None])

    second_other = to_sibling(second_weight)
    cot = cotangent.reshape(HALF, 2, PLANE)
    cot_own = jnp.where(even, cot[:, 0], cot[:, 1])
    cot_other = to_sibling(jnp.where(even, cot[:, 1], cot[:, 0]))
    features_far = to_sibling(jnp.where(even, prev, following))

    prev, following = halos(hidden)
    hidden_near = (prev, hidden, following)
    output, grad_second = conv_call(
        second_kernel,
        [struct((CH, PLANE)), struct((CH, PLANE))],
        3,
        [pltpu.VMEM((CH, PLANE), BF)],
        "second",
    )(pos, *hidden_near, second_weight, second_other, biases[1][:, None], cot_own, cot_other)
    hidden_far = to_sibling(jnp.where(even, prev, following))

    prev, following = halos(grad_second)
    grad_other = to_sibling(jnp.where(even, grad_second[HALF:], grad_second[:HALF]))
    grad_first = conv_call(hidden_grad_kernel, struct((CH, PLANE)), 1, [], "hidden_grad")(
        pos, prev, grad_second, following, second_weight, second_other, first_sum
    )
    second_terms = weight_terms(pos, hidden_near, hidden_far, grad_second, grad_other, "second_terms")

    grad_other = to_sibling(jnp.where(even, grad_first[HALF:], grad_first[:HALF]))
    first_terms = weight_terms(pos, features_near, features_far, grad_first, grad_other, "first_terms")
    prev, following = halos(grad_first)
    input_grad = conv_call(input_grad_kernel, struct((CH, PLANE)), 0, [], "input_grad")(
        pos, prev, grad_first, following, first_weight, first_other
    )

    voxels = 2 * PLANE * lax.axis_size("slab")
    first_out, second_out, first_bias_out, second_bias_out = reduced(
        pos, first_terms, second_terms, 1.0 / math.sqrt(voxels)
    )

    kept = jnp.where(even, output[:HALF], output[HALF:])
    came = to_sibling(jnp.where(even, output[HALF:], output[:HALF]))
    output = jnp.where(even, jnp.stack([kept, came], axis=1), jnp.stack([came, kept], axis=1))
    cut = 2 * LANES
    kept = jnp.where(even, input_grad[:, :cut], input_grad[:, cut:])
    came = to_sibling(jnp.where(even, input_grad[:, cut:], input_grad[:, :cut]))
    input_grad = jnp.where(even, jnp.stack([kept, came], axis=1), jnp.stack([came, kept], axis=1))
    shape = (3, 3, 3, HALF, CH)
    return (
        output.reshape(HALF, 2, 4, LANES),
        input_grad.reshape(CH, 2, 2, LANES),
        first_out.reshape(shape),
        first_bias_out[:, 0],
        second_out.reshape(shape),
        second_bias_out[:, 0],
    )


def solution(mesh):
    placed = (
        P(None, "slab", "chan", None),
        P(None, None, None, "chan", None),
        P("chan"),
        P(None, None, None, "chan", None),
        P("chan"),
        P("chan", "slab", None, None),
    )
    return jax.shard_map(
        per_device,
        mesh=mesh,
        in_specs=placed,
        out_specs=(
            P("chan", "slab", None, None),
            P(None, "slab", "chan", None),
            P(None, None, None, "chan", None),
            P("chan"),
            P(None, None, None, "chan", None),
            P("chan"),
        ),
        check_vma=False,
    )
```

```python
import functools
import math

import jax
import jax.numpy as jnp
from jax import lax
from jax.experimental import pallas as pl
from jax.experimental.pallas import tpu as pltpu
from jax.sharding import PartitionSpec as P

BF = jnp.bfloat16
F32 = jnp.float32
AXES = ("slab", "chan")
CH = 256
HALF = 128
LANES = 128
PLANE = 512
TAPS = 27
X, Y, Z = 4, 4, 8
DEVICES = 2 * X * Y * Z
ROWS = 28 * HALF
PIECE = 112
GROUPS = 3
ORDERS = ((0, 1, 3, 2), (0, 3, 1, 2))
STREAMS = ((True, ORDERS[0]), (True, ORDERS[1]), (False, ORDERS[0]), (False, ORDERS[1]))
VMEM = pl.BlockSpec(memory_space=pltpu.VMEM)
SMEM = pl.BlockSpec(memory_space=pltpu.SMEM)
ANY = pl.BlockSpec(memory_space=pl.ANY)


def call(kernel, out_shape, in_specs, scratch, flops, moved, name, room=18, out_specs=None):
    return pl.pallas_call(
        kernel,
        out_shape=out_shape,
        in_specs=in_specs,
        out_specs=jax.tree.map(lambda _: VMEM, out_shape) if out_specs is None else out_specs,
        scratch_shapes=scratch,
        compiler_params=pltpu.CompilerParams(vmem_limit_bytes=room * 2**20),
        cost_estimate=pl.CostEstimate(flops=flops, bytes_accessed=moved, transcendentals=0),
        name=name,
    )


def struct(shape, dtype=BF):
    return jax.ShapeDtypeStruct(shape, dtype)


def place(slab):
    return slab % X, (slab // X) % Y, slab // (X * Y)


def slab_of(x, y, z):
    return (z * Y + y) * X + x


def move(value, target):
    pairs = []
    for line in range(DEVICES):
        to = target(line)
        if 0 <= to < DEVICES:
            pairs.append((line, to))
    return lax.ppermute(value, AXES, pairs)


def to_sibling(value):
    return move(value, lambda line: line ^ 1)


def to_neighbour(value):
    return move(value, lambda line: line + 1 if line % 2 else line - 1)


def across(value, axis, mask):
    def target(line):
        x, y, z = place(line // 2)
        if axis == "x":
            x = x ^ mask
        elif axis == "y":
            y = y ^ mask
        else:
            z = z ^ mask
        return slab_of(x, y, z) * 2 + line % 2

    return move(value, target)


def tied(one, two):
    return lax.optimization_barrier((one, two))


def shifted(plane, tap):
    if tap == 1:
        return plane
    wide = plane.astype(F32)
    lane = lax.broadcasted_iota(jnp.int32, (wide.shape[0], LANES), 1)
    parts = []
    for row in range(PLANE // LANES):
        part = wide[:, row * LANES : (row + 1) * LANES]
        if tap == 0:
            part = jnp.where(lane == 0, 0.0, pltpu.roll(part, 1, 1))
        else:
            part = jnp.where(lane == LANES - 1, 0.0, pltpu.roll(part, LANES - 1, 1))
        parts.append(part.astype(BF))
    return jnp.concatenate(parts, axis=1)


def fill(views, index, plane):
    zero = jnp.zeros((CH, LANES), BF)
    for tap in range(3):
        views[tap, index, :, 0:LANES] = zero
        views[tap, index, :, LANES + PLANE :] = zero
        views[tap, index, :, LANES : LANES + PLANE] = shifted(plane, tap)


def half(index, width):
    return pl.ds(pl.multiple_of(index * width, width), width)


def taps():
    return [(x, z, y) for x in range(3) for z in range(3) for y in range(3)]


def own_first(core, plane):
    return jnp.concatenate([plane[half(core, HALF), :], plane[half(1 - core, HALF), :]], axis=0)


def put_halves(core, target, value):
    target[half(core, HALF), :] = value[:HALF]
    target[half(1 - core, HALF), :] = value[HALF:]


def products(weights, views, planes, back):
    total = None
    for index, x in planes:
        for z in range(3):
            for y in range(3):
                tap = x * 9 + z * 3 + y
                if back:
                    tap = TAPS - 1 - tap
                both = jnp.concatenate([weights[0][tap], weights[1][tap]], axis=0)
                term = lax.dot_general(
                    both,
                    views[y, index, :, z * LANES : z * LANES + PLANE],
                    (((0 if back else 1,), (0,)), ((), ())),
                    preferred_element_type=F32,
                )
                total = term if total is None else total + term
    return total


def chip_planes(core):
    return (0, 1), (1, 2 - 2 * core)


def far_plane(core):
    return ((0, 2 * core),)


def sigmoid(value):
    return 1.0 / (1.0 + jnp.exp(-value))


def slope(value):
    sig = sigmoid(value)
    return sig * (1.0 + value * (1.0 - sig))


def bias_column(own, other):
    rows = [jnp.broadcast_to(part[...], (HALF, LANES)).T for part in (own, other)]
    return jnp.concatenate([jnp.concatenate(rows, axis=0)] * (PLANE // LANES), axis=1)


def put_parts(core, plane, mine, theirs):
    plane[:, half(core, 2 * LANES)] = mine
    plane[:, half(1 - core, 2 * LANES)] = theirs


def first_chip_kernel(pos, feats, feats_other, w_own, w_other, partial, views, plane):
    core = pos[0]
    for index, part in enumerate((core, 1 - core)):
        lanes = half(part, 2 * LANES)
        put_parts(core, plane, feats[:, lanes], feats_other[:, lanes])
        fill(views, index, plane[...])
    partial[...] = products((w_own, w_other), views, chip_planes(core), False)


def first_kernel(
    pos, partial, near, far, w_own, w_other, bias, bias_other, sums, hidden, views, plane
):
    core = pos[0]
    put_parts(core, plane, far[...], near[...])
    fill(views, 0, plane[...])
    value = partial[...] + products((w_own, w_other), views, far_plane(core), False) + bias_column(bias, bias_other)
    put_halves(core, sums, value)
    put_halves(core, hidden, (value * sigmoid(value)).astype(BF))


def chip_kernel(back, pos, own, sibling, w_own, w_other, partial, views):
    core = pos[0]
    for index, plane in enumerate((own, sibling)):
        fill(views, index, own_first(core, plane) if back else plane[...])
    partial[...] = products((w_own, w_other), views, chip_planes(core), back)


def second_kernel(
    pos, partial, neighbour, w_own, w_other, bias, bias_other, cots, cots_other, output, grad, views
):
    core = pos[0]
    fill(views, 0, neighbour[...])
    value = partial[...] + products((w_own, w_other), views, far_plane(core), False) + bias_column(bias, bias_other)
    put_halves(core, output, (value * sigmoid(value)).astype(BF))
    lanes = half(core, PLANE)
    cot = jnp.concatenate([cots[:, lanes], cots_other[:, lanes]], axis=0)
    put_halves(core, grad, (cot.astype(F32) * slope(value)).astype(BF))


def hidden_grad_kernel(pos, partial, neighbour, w_own, w_other, sums, grad, views):
    core = pos[0]
    fill(views, 0, own_first(core, neighbour))
    value = partial[...] + products((w_own, w_other), views, far_plane(core), True)
    grad[...] = (value * slope(sums[...])).astype(BF)


def input_grad_kernel(pos, partial, neighbour, w_own, w_other, grad, views):
    core = pos[0]
    fill(views, 0, own_first(core, neighbour))
    value = partial[...] + products((w_own, w_other), views, far_plane(core), True)
    grad[...] = value.astype(BF)


def arrange_kernel(pos, out, out_other, grad, grad_other, out_placed, grad_placed):
    core = pos[0]
    rows, lanes = half(core, HALF), half(core, 2 * LANES)
    out_placed[:, half(core, PLANE)] = out[rows, :]
    out_placed[:, half(1 - core, PLANE)] = out_other[rows, :]
    grad_placed[:, lanes] = grad[:, lanes]
    grad_placed[:, half(1 - core, 2 * LANES)] = grad_other[:, lanes]


CONV_FLOPS = 2 * TAPS * CH * CH * PLANE


def conv_call(kernel, out_shape, operands, planes, scratch, name):
    return call(
        kernel,
        out_shape,
        [SMEM] + [VMEM] * operands,
        [pltpu.VMEM((3, planes, CH, PLANE + 2 * LANES), BF)] + scratch,
        CONV_FLOPS * planes // 3,
        6 * 2**20,
        name,
    )


def chunk_of(pos, stream, outer, inner):
    first_x, order = STREAMS[stream]
    mx, my = (order[outer], inner) if first_x else (inner, order[outer])
    return (pos[2] ^ my) * X + (pos[1] ^ mx)


def term_rows(pos, own, sibling, neighbour, far, grad_own, grad_sibling, rows, views, grads):
    core = pos[0]
    fill(views, 1 + core, own[...])
    fill(views, 2 - core, sibling[...])
    fill(views, 3 * core, neighbour[...])
    fill(views, 3 - 3 * core, far[...])
    grad_rows(core, grad_own, grad_sibling, rows, views, grads)


def grad_rows(core, grad_own, grad_sibling, rows, views, grads):
    grads[core] = grad_own[half(core, HALF), :]
    grads[1 - core] = grad_sibling[half(core, HALF), :]
    one, two = grads[0], grads[1]
    for x, z, y in taps():
        tap = x * 9 + z * 3 + y
        total = None
        for index, grad in enumerate((one, two)):
            term = lax.dot_general(
                grad,
                views[y, x + index, :, z * LANES : z * LANES + PLANE],
                (((1,), (1,)), ((), ())),
                preferred_element_type=F32,
            )
            total = term if total is None else total + term
        total = total.astype(BF)
        rows[tap * HALF : (tap + 1) * HALF, :] = total[:, :HALF]
        rows[ROWS + tap * HALF : ROWS + (tap + 1) * HALF, :] = total[:, HALF:]
    bias = jnp.zeros((HALF, LANES), F32)
    for grad in (one, two):
        for row in range(PLANE // LANES):
            bias = bias + grad[:, row * LANES : (row + 1) * LANES].astype(F32)
    rows[TAPS * HALF : ROWS, :] = bias.astype(BF)
    rows[ROWS + TAPS * HALF :, :] = jnp.zeros((HALF, LANES), BF)


def first_terms_kernel(
    pos, feats, feats_other, near, far, near_other, far_other, grad_own, grad_sibling, others,
    s0, s1, s2, s3, k0, k1, k2, k3, views, grads, rows, plane
):
    core = pos[0]
    for index, part in ((1 + core, core), (2 - core, 1 - core)):
        lanes = half(part, 2 * LANES)
        put_parts(core, plane, feats[:, lanes], feats_other[:, lanes])
        fill(views, index, plane[...])
    put_parts(core, plane, far[...], near[...])
    fill(views, 3 * core, plane[...])
    put_parts(core, plane, near_other[...], far_other[...])
    fill(views, 3 - 3 * core, plane[...])
    grad_rows(core, grad_own, grad_sibling, rows, views, grads)
    sends, keeps = (s0, s1, s2, s3), (k0, k1, k2, k3)
    for weight, source in enumerate((rows, others)):
        for stream in range(4):
            for outer in range(4):
                for inner in range(4):
                    start = chunk_of(pos, stream, outer, inner) * (4 * PIECE) + stream * PIECE
                    target = keeps[stream] if outer < 2 else sends[stream]
                    target[(outer % 2) * 4 + inner, weight] = source[
                        pl.ds(pl.multiple_of(start, 16), PIECE), :
                    ]


TERM_SCRATCH = [
    pltpu.VMEM((3, 4, CH, PLANE + 2 * LANES), BF),
    pltpu.VMEM((2, HALF, PLANE), BF),
]


def added(one, two):
    return (one.astype(F32) + two.astype(F32)).astype(BF)


def outer_kernel(*refs):
    for stream in range(4):
        kept, came, send, keep = (refs[4 * i + stream] for i in range(4))
        keep[...] = added(kept[0:4], came[0:4])
        send[...] = added(kept[4:8], came[4:8])


def inner_kernel(*refs):
    targets = refs[8:16]
    for stream in range(4):
        kept, came = refs[stream], refs[4 + stream]
        for inner in range(4):
            for weight in range(2):
                targets[stream // 2 * 4 + inner][weight * 2 + stream % 2] = added(
                    kept[inner, weight], came[inner, weight]
                )


def depth_kernel(pos, *refs):
    send, keep, work = refs[8:]
    for group in range(2):
        for weight in range(2):
            for part in range(2):
                total = None
                for ref in refs[4 * group : 4 * group + 4]:
                    term = ref[weight * 2 + part].astype(F32)
                    total = term if total is None else total + term
                work[weight * 4 + group * 2 + part] = total.astype(BF)
    for slot in range(4):
        keep[slot] = work[2 * slot + pos[3] % 2]
        send[slot] = work[2 * slot + 1 - pos[3] % 2]


def add_kernel(one, two, out):
    out[...] = added(one[...], two[...])


def ring_kernel(pos, c0, c2, c4, c6, out, work):
    for index, term in enumerate((c0, c2, c4, c6)):
        work[pos[3] // 2 ^ index] = term[...]
    total = work[0].astype(F32)
    for index in range(1, 4):
        total = total + work[index].astype(F32)
    out[...] = total.astype(BF)


def gather_kernel(*refs):
    for group in range(2):
        for inner in range(4):
            for part in range(2):
                refs[8 + group * 2 + part][inner] = refs[4 * group + inner][2 * part : 2 * part + 2]


def join_kernel(*refs):
    for stream in range(4):
        refs[8 + stream][0:4] = refs[stream][...]
        refs[8 + stream][4:8] = refs[4 + stream][...]


def final_kernel(scale, pos, *refs):
    held, came = refs[0:4], refs[4:8]
    first, second, first_bias, second_bias, rows, ready, sems = refs[8:]
    for stream in range(4):
        for outer in range(4):
            for inner in range(4):
                chunk = chunk_of(pos, stream, outer, inner)
                source = held[stream] if outer < 2 else came[stream]
                for part in range(2):
                    index = 2 * (2 * (stream % 2) + part) + (pos[3] % 2 ^ (stream // 2))
                    start = chunk * (4 * PIECE) + (index % 4) * PIECE
                    rows[index // 4, pl.ds(pl.multiple_of(start, 16), PIECE), :] = source[
                        (outer % 2) * 4 + inner, part
                    ]
    ones = jnp.ones((8, LANES), BF)
    copies = []
    for weight, (target, bias) in enumerate(((first, first_bias), (second, second_bias))):
        for group in range(GROUPS):
            part = slice(group * TAPS // GROUPS, (group + 1) * TAPS // GROUPS)
            for tap in range(part.start, part.stop):
                for side in range(2):
                    start = side * ROWS + tap * HALF
                    ready[weight, tap, :, side * HALF : (side + 1) * HALF] = (
                        rows[weight, start : start + HALF, :].astype(F32) * scale
                    )
            copy = pltpu.make_async_copy(
                ready.at[weight, part], target.at[part], sems.at[weight, group]
            )
            copy.start()
            copies.append(copy)
        sums = lax.dot_general(
            ones,
            rows[weight, TAPS * HALF : ROWS, :],
            (((1,), (1,)), ((), ())),
            preferred_element_type=F32,
        )
        bias[...] = sums[0:1] * scale
    for copy in copies:
        copy.wait()


def outer_axis(stream):
    return "x" if STREAMS[stream][0] else "y"


def swap_outer(values, place_in_order):
    return [
        across(value, outer_axis(stream), STREAMS[stream][1][place_in_order])
        for stream, value in enumerate(values)
    ]


def inner_axis(group):
    return "y" if group == 0 else "x"


def per_device(features, first_weight, first_bias, second_weight, second_bias, cotangent):
    core = lax.axis_index("chan")
    even = core == 0
    x, y, z = place(lax.axis_index("slab"))
    pos = jnp.stack([core, x, y, z]).astype(jnp.int32)
    first_weight = first_weight.reshape(TAPS, HALF, CH)
    second_weight = second_weight.reshape(TAPS, HALF, CH)
    plane, sums = struct((CH, PLANE)), struct((CH, PLANE), F32)

    feats = features.reshape(CH, PLANE)
    cut = 2 * LANES
    near = to_neighbour(jnp.where(even, feats[:, :cut], feats[:, cut:]))
    far = move(
        jnp.where(even, feats[:, cut:], feats[:, :cut]),
        lambda line: line - 2 if line % 2 else line + 2,
    )
    feats_other = to_sibling(feats)
    first_other = to_sibling(first_weight)
    first_bias, second_bias = first_bias[None], second_bias[None]
    first_bias_other, second_bias_other = to_sibling(first_bias), to_sibling(second_bias)
    partial = conv_call(first_chip_kernel, sums, 4, 2, [pltpu.VMEM((CH, PLANE), BF)], "first_chip")(
        pos, feats, feats_other, first_weight, first_other
    )
    (near, far), partial = tied((near, far), partial)
    first_sum, hidden = conv_call(
        first_kernel, [sums, plane], 7, 1, [pltpu.VMEM((CH, PLANE), BF)], "first"
    )(pos, partial, near, far, first_weight, first_other, first_bias, first_bias_other)

    def chip_part(back, own, sibling, weight, other):
        kernel = functools.partial(chip_kernel, back)
        return conv_call(kernel, sums, 4, 2, [], "chip_back" if back else "chip")(
            pos, own, sibling, weight, other
        )

    second_other = to_sibling(second_weight)
    cots = cotangent.reshape(HALF, 2 * PLANE)
    cots_other = to_sibling(cots)
    near_other, far_other = to_sibling(near), to_sibling(far)
    hidden_sibling, hidden_neighbour = to_sibling(hidden), to_neighbour(hidden)
    partial = chip_part(False, hidden, hidden_sibling, second_weight, second_other)
    hidden_neighbour, partial = tied(hidden_neighbour, partial)
    hidden_near = (hidden, hidden_sibling, hidden_neighbour)
    output, grad_second = conv_call(second_kernel, [plane, plane], 8, 1, [], "second")(
        pos,
        partial,
        hidden_neighbour,
        second_weight,
        second_other,
        second_bias,
        second_bias_other,
        cots,
        cots_other,
    )
    hidden_far = to_sibling(hidden_near[2])

    grad_sibling, grad_neighbour = to_sibling(grad_second), to_neighbour(grad_second)
    second_rows = call(
        term_rows,
        struct((2 * ROWS, LANES)),
        [SMEM] + [VMEM] * 6,
        TERM_SCRATCH,
        CONV_FLOPS,
        5 * 2**20,
        "second_terms",
    )
    second_rows = second_rows(pos, *hidden_near, hidden_far, grad_second, grad_sibling)
    second_rows, grad_sibling = tied(second_rows, grad_sibling)
    partial = chip_part(True, grad_second, grad_sibling, second_weight, second_other)
    grad_neighbour, partial = tied(grad_neighbour, partial)
    grad_first = conv_call(hidden_grad_kernel, plane, 5, 1, [], "hidden_grad")(
        pos, partial, grad_neighbour, second_weight, second_other, first_sum
    )

    grad_sibling, grad_neighbour = to_sibling(grad_first), to_neighbour(grad_first)
    halves = struct((8, 2, PIECE, LANES))
    terms = call(
        first_terms_kernel,
        [halves] * 8,
        [SMEM] + [VMEM] * 9,
        TERM_SCRATCH + [pltpu.VMEM((2 * ROWS, LANES), BF), pltpu.VMEM((CH, PLANE), BF)],
        CONV_FLOPS,
        9 * 2**20,
        "first_terms",
    )(
        pos, feats, feats_other, near, far, near_other, far_other, grad_first, grad_sibling, second_rows
    )

    came = swap_outer(terms[:4], 2)
    partial = chip_part(True, grad_first, grad_sibling, first_weight, first_other)
    input_grad = conv_call(input_grad_kernel, plane, 4, 1, [], "input_grad")(
        pos, partial, grad_neighbour, first_weight, first_other
    )
    came, input_grad = tied(came, input_grad)
    quarters = struct((4, 2, PIECE, LANES))
    halved = call(outer_kernel, [quarters] * 8, [VMEM] * 8, [], 2**21, 7 * 2**20, "outer")(
        *terms[4:], *came
    )
    came = swap_outer(halved[:4], 1)
    out_placed, grad_placed = call(
        arrange_kernel,
        [struct((HALF, 2 * PLANE)), plane],
        [SMEM] + [VMEM] * 4,
        [],
        2**18,
        2**20,
        "arrange",
    )(pos, output, to_sibling(output), input_grad, to_sibling(input_grad))
    out_placed = out_placed.reshape(HALF, 2, 4, LANES)
    grad_placed = grad_placed.reshape(CH, 2, 2, LANES)
    came, (out_placed, grad_placed) = tied(came, (out_placed, grad_placed))
    pieces = struct((4, PIECE, LANES))
    spread = call(inner_kernel, [pieces] * 8, [VMEM] * 8, [], 2**20, 4 * 2**20, "inner")(
        *halved[4:], *came
    )
    groups = []
    for group in range(2):
        groups.append(spread[4 * group])
        for mask in range(1, 4):
            groups.append(across(spread[4 * group + mask], inner_axis(group), mask))
    send, keep = call(
        depth_kernel,
        [pieces] * 2,
        [SMEM] + [VMEM] * 8,
        [pltpu.VMEM((8, PIECE, LANES), BF)],
        2**19,
        2**20,
        "depth",
    )(pos, *groups)
    came = across(send, "z", 1)
    held = call(add_kernel, pieces, [VMEM] * 2, [], 2**17, 2**18, "add")(keep, came)
    held = call(
        ring_kernel,
        pieces,
        [SMEM] + [VMEM] * 4,
        [pltpu.VMEM((4, 4, PIECE, LANES), BF)],
        2**18,
        2**19,
        "ring",
    )(pos, held, *[across(held, "z", mask) for mask in (2, 4, 6)])

    groups = []
    for group, value in enumerate((held, across(held, "z", 1))):
        groups += [value] + [across(value, inner_axis(group), mask) for mask in range(1, 4)]
    held = call(gather_kernel, [quarters] * 4, [VMEM] * 8, [], 2**18, 4 * 2**20, "gather")(*groups)
    came = swap_outer(held, 1)
    held = call(join_kernel, [halves] * 4, [VMEM] * 8, [], 2**18, 4 * 2**20, "join")(*held, *came)
    came = swap_outer(held, 2)
    scale = 1.0 / math.sqrt(2 * PLANE * lax.axis_size("slab"))
    whole = struct((TAPS, HALF, CH), F32)
    line = struct((1, HALF), F32)
    first_out, second_out, first_bias_out, second_bias_out = call(
        functools.partial(final_kernel, scale),
        [whole, whole, line, line],
        [SMEM] + [VMEM] * 8,
        [
            pltpu.VMEM((2, 2 * ROWS, LANES), BF),
            pltpu.VMEM((2, TAPS, HALF, CH), F32),
            pltpu.SemaphoreType.DMA((2, GROUPS)),
        ],
        2**22,
        12 * 2**20,
        "final",
        out_specs=[ANY, ANY, VMEM, VMEM],
    )(pos, *held, *came)
    shape = (3, 3, 3, HALF, CH)
    return (
        out_placed,
        grad_placed,
        first_out.reshape(shape),
        first_bias_out[0],
        second_out.reshape(shape),
        second_bias_out[0],
    )


def solution(mesh):
    placed = (
        P(None, "slab", "chan", None),
        P(None, None, None, "chan", None),
        P("chan"),
        P(None, None, None, "chan", None),
        P("chan"),
        P("chan", "slab", None, None),
    )
    return jax.shard_map(
        per_device,
        mesh=mesh,
        in_specs=placed,
        out_specs=(
            P("chan", "slab", None, None),
            P(None, "slab", "chan", None),
            P(None, None, None, "chan", None),
            P("chan"),
            P(None, None, None, "chan", None),
            P("chan"),
        ),
        check_vma=False,
    )
```

```python
import functools
import math

import jax
import jax.numpy as jnp
from jax import lax
from jax.experimental import pallas as pl
from jax.experimental.pallas import tpu as pltpu
from jax.sharding import PartitionSpec as P

BF = jnp.bfloat16
F32 = jnp.float32
AXES = ("slab", "chan")
CH = 256
HALF = 128
LANES = 128
PLANE = 512
TAPS = 27
X, Y, Z = 4, 4, 8
DEVICES = 2 * X * Y * Z
ROWS = 28 * HALF
PIECE = 112
GROUPS = 3
GROUP_AXES = (("x", "y"), ("y", "x"))
MASKS = (2, 1, 3)
VMEM = pl.BlockSpec(memory_space=pltpu.VMEM)
SMEM = pl.BlockSpec(memory_space=pltpu.SMEM)
ANY = pl.BlockSpec(memory_space=pl.ANY)
HBM = pl.BlockSpec(memory_space=pltpu.HBM)


def call(kernel, out_shape, in_specs, scratch, flops, moved, name, room=18, out_specs=None):
    return pl.pallas_call(
        kernel,
        out_shape=out_shape,
        in_specs=in_specs,
        out_specs=jax.tree.map(lambda _: VMEM, out_shape) if out_specs is None else out_specs,
        scratch_shapes=scratch,
        compiler_params=pltpu.CompilerParams(vmem_limit_bytes=room * 2**20),
        cost_estimate=pl.CostEstimate(flops=flops, bytes_accessed=moved, transcendentals=0),
        name=name,
    )


def struct(shape, dtype=BF):
    return jax.ShapeDtypeStruct(shape, dtype)


def place(slab):
    return slab % X, (slab // X) % Y, slab // (X * Y)


def slab_of(x, y, z):
    return (z * Y + y) * X + x


def move(value, target):
    pairs = []
    for line in range(DEVICES):
        to = target(line)
        if 0 <= to < DEVICES:
            pairs.append((line, to))
    return lax.ppermute(value, AXES, pairs)


def to_sibling(value):
    return move(value, lambda line: line ^ 1)


def to_neighbour(value):
    return move(value, lambda line: line + 1 if line % 2 else line - 1)


def across(value, axis, mask):
    def target(line):
        x, y, z = place(line // 2)
        if axis == "x":
            x = x ^ mask
        elif axis == "y":
            y = y ^ mask
        else:
            z = z ^ mask
        return slab_of(x, y, z) * 2 + line % 2

    return move(value, target)


def tied(one, two):
    return lax.optimization_barrier((one, two))


def shifted(plane, tap):
    if tap == 1:
        return plane
    wide = plane.astype(F32)
    lane = lax.broadcasted_iota(jnp.int32, (wide.shape[0], LANES), 1)
    parts = []
    for row in range(PLANE // LANES):
        part = wide[:, row * LANES : (row + 1) * LANES]
        if tap == 0:
            part = jnp.where(lane == 0, 0.0, pltpu.roll(part, 1, 1))
        else:
            part = jnp.where(lane == LANES - 1, 0.0, pltpu.roll(part, LANES - 1, 1))
        parts.append(part.astype(BF))
    return jnp.concatenate(parts, axis=1)


def fill(views, index, plane):
    zero = jnp.zeros((CH, LANES), BF)
    for tap in range(3):
        views[tap, index, :, 0:LANES] = zero
        views[tap, index, :, LANES + PLANE :] = zero
        views[tap, index, :, LANES : LANES + PLANE] = shifted(plane, tap)


def half(index, width):
    return pl.ds(pl.multiple_of(index * width, width), width)


def taps():
    return [(x, z, y) for x in range(3) for z in range(3) for y in range(3)]


def own_first(core, plane):
    return jnp.concatenate([plane[half(core, HALF), :], plane[half(1 - core, HALF), :]], axis=0)


def put_halves(core, target, value):
    target[half(core, HALF), :] = value[:HALF]
    target[half(1 - core, HALF), :] = value[HALF:]


def products(weights, views, planes, back):
    total = None
    for index, x in planes:
        for z in range(3):
            for y in range(3):
                tap = x * 9 + z * 3 + y
                if back:
                    tap = TAPS - 1 - tap
                both = jnp.concatenate([weights[0][tap], weights[1][tap]], axis=0)
                term = lax.dot_general(
                    both,
                    views[y, index, :, z * LANES : z * LANES + PLANE],
                    (((0 if back else 1,), (0,)), ((), ())),
                    preferred_element_type=F32,
                )
                total = term if total is None else total + term
    return total


def fetch(w_own, w_other, weights, sems):
    copies = [
        pltpu.make_async_copy(source, weights.at[index], sems.at[index])
        for index, source in enumerate((w_own, w_other))
    ]
    for copy in copies:
        copy.start()
    return copies


def chip_planes(core):
    return (0, 1), (1, 2 - 2 * core)


def far_plane(core):
    return ((0, 2 * core),)


def sigmoid(value):
    return 1.0 / (1.0 + jnp.exp(-value))


def slope(value):
    sig = sigmoid(value)
    return sig * (1.0 + value * (1.0 - sig))


def bias_column(own, other):
    rows = [jnp.broadcast_to(part[...], (HALF, LANES)).T for part in (own, other)]
    return jnp.concatenate([jnp.concatenate(rows, axis=0)] * (PLANE // LANES), axis=1)


def put_parts(core, plane, mine, theirs):
    plane[:, half(core, 2 * LANES)] = mine
    plane[:, half(1 - core, 2 * LANES)] = theirs


def first_chip_kernel(
    pos, feats, feats_other, w_own, w_other, partial, views, weights, sems, plane
):
    core = pos[0]
    copies = fetch(w_own, w_other, weights, sems)
    for index, part in enumerate((core, 1 - core)):
        lanes = half(part, 2 * LANES)
        put_parts(core, plane, feats[:, lanes], feats_other[:, lanes])
        fill(views, index, plane[...])
    for copy in copies:
        copy.wait()
    partial[...] = products((weights.at[0], weights.at[1]), views, chip_planes(core), False)


def first_kernel(
    pos, partial, near, far, w_own, w_other, bias, bias_other, sums, hidden, views, plane
):
    core = pos[0]
    put_parts(core, plane, far[...], near[...])
    fill(views, 0, plane[...])
    value = partial[...] + products((w_own, w_other), views, far_plane(core), False) + bias_column(bias, bias_other)
    put_halves(core, sums, value)
    put_halves(core, hidden, (value * sigmoid(value)).astype(BF))


def chip_kernel(back, pos, own, sibling, w_own, w_other, partial, views, weights, sems):
    core = pos[0]
    copies = fetch(w_own, w_other, weights, sems)
    for index, plane in enumerate((own, sibling)):
        fill(views, index, own_first(core, plane) if back else plane[...])
    for copy in copies:
        copy.wait()
    partial[...] = products((weights.at[0], weights.at[1]), views, chip_planes(core), back)


def second_kernel(
    pos, partial, neighbour, w_own, w_other, bias, bias_other, cots, cots_other, output, grad, views
):
    core = pos[0]
    fill(views, 0, neighbour[...])
    value = partial[...] + products((w_own, w_other), views, far_plane(core), False) + bias_column(bias, bias_other)
    put_halves(core, output, (value * sigmoid(value)).astype(BF))
    lanes = half(core, PLANE)
    cot = jnp.concatenate([cots[:, lanes], cots_other[:, lanes]], axis=0)
    put_halves(core, grad, (cot.astype(F32) * slope(value)).astype(BF))


def hidden_grad_kernel(pos, partial, neighbour, w_own, w_other, sums, grad, views):
    core = pos[0]
    fill(views, 0, own_first(core, neighbour))
    value = partial[...] + products((w_own, w_other), views, far_plane(core), True)
    grad[...] = (value * slope(sums[...])).astype(BF)


def input_grad_kernel(pos, partial, neighbour, w_own, w_other, grad, views):
    core = pos[0]
    fill(views, 0, own_first(core, neighbour))
    value = partial[...] + products((w_own, w_other), views, far_plane(core), True)
    grad[...] = value.astype(BF)


def arrange_kernel(pos, out, out_other, grad, grad_other, out_placed, grad_placed):
    core = pos[0]
    rows, lanes = half(core, HALF), half(core, 2 * LANES)
    out_placed[:, half(core, PLANE)] = out[rows, :]
    out_placed[:, half(1 - core, PLANE)] = out_other[rows, :]
    grad_placed[:, lanes] = grad[:, lanes]
    grad_placed[:, half(1 - core, 2 * LANES)] = grad_other[:, lanes]


CONV_FLOPS = 2 * TAPS * CH * CH * PLANE


def conv_call(kernel, out_shape, operands, planes, scratch, name):
    specs = [VMEM] * operands
    fetched = []
    if planes == 2:
        specs[2:4] = [HBM, HBM]
        fetched = [pltpu.VMEM((2, TAPS, HALF, CH), BF), pltpu.SemaphoreType.DMA((2,))]
    return call(
        kernel,
        out_shape,
        [SMEM] + specs,
        [pltpu.VMEM((3, planes, CH, PLANE + 2 * LANES), BF)] + fetched + scratch,
        CONV_FLOPS * planes // 3,
        6 * 2**20,
        name,
        room=13,
    )


def chunk_of(pos, group, outer, inner):
    mx, my = (outer, inner) if GROUP_AXES[group][0] == "x" else (inner, outer)
    return (pos[2] ^ my) * X + (pos[1] ^ mx)


def rows_of(pos, group, outer, inner, part):
    start = chunk_of(pos, group, outer, inner) * (4 * PIECE) + (2 * group + part) * PIECE
    return pl.ds(pl.multiple_of(start, 16), PIECE)


def term_rows(pos, own, sibling, neighbour, far, grad_own, grad_sibling, rows, views, grads):
    core = pos[0]
    fill(views, 1 + core, own[...])
    fill(views, 2 - core, sibling[...])
    fill(views, 3 * core, neighbour[...])
    fill(views, 3 - 3 * core, far[...])
    grad_rows(core, grad_own, grad_sibling, rows, views, grads)


def grad_rows(core, grad_own, grad_sibling, rows, views, grads):
    grads[core] = grad_own[half(core, HALF), :]
    grads[1 - core] = grad_sibling[half(core, HALF), :]
    one, two = grads[0], grads[1]
    for x, z, y in taps():
        tap = x * 9 + z * 3 + y
        total = None
        for index, grad in enumerate((one, two)):
            term = lax.dot_general(
                grad,
                views[y, x + index, :, z * LANES : z * LANES + PLANE],
                (((1,), (1,)), ((), ())),
                preferred_element_type=F32,
            )
            total = term if total is None else total + term
        total = total.astype(BF)
        rows[tap * HALF : (tap + 1) * HALF, :] = total[:, :HALF]
        rows[ROWS + tap * HALF : ROWS + (tap + 1) * HALF, :] = total[:, HALF:]
    bias = jnp.zeros((HALF, LANES), F32)
    for grad in (one, two):
        for row in range(PLANE // LANES):
            bias = bias + grad[:, row * LANES : (row + 1) * LANES].astype(F32)
    rows[TAPS * HALF : ROWS, :] = bias.astype(BF)
    rows[ROWS + TAPS * HALF :, :] = jnp.zeros((HALF, LANES), BF)


def first_terms_kernel(
    pos, feats, feats_other, near, far, near_other, far_other, grad_own, grad_sibling, others,
    a0, a1, a2, a3, b0, b1, b2, b3, views, grads, rows, plane
):
    core = pos[0]
    for index, part in ((1 + core, core), (2 - core, 1 - core)):
        lanes = half(part, 2 * LANES)
        put_parts(core, plane, feats[:, lanes], feats_other[:, lanes])
        fill(views, index, plane[...])
    put_parts(core, plane, far[...], near[...])
    fill(views, 3 * core, plane[...])
    put_parts(core, plane, near_other[...], far_other[...])
    fill(views, 3 - 3 * core, plane[...])
    grad_rows(core, grad_own, grad_sibling, rows, views, grads)
    for weight, source in enumerate((rows, others)):
        for group, targets in enumerate(((a0, a1, a2, a3), (b0, b1, b2, b3))):
            for outer in range(4):
                for inner in range(4):
                    for part in range(2):
                        targets[outer][inner, weight * 2 + part] = source[
                            rows_of(pos, group, outer, inner, part), :
                        ]


TERM_SCRATCH = [
    pltpu.VMEM((3, 4, CH, PLANE + 2 * LANES), BF),
    pltpu.VMEM((2, HALF, PLANE), BF),
]


def added(one, two):
    return (one.astype(F32) + two.astype(F32)).astype(BF)


def outer_kernel(*refs):
    for group in range(2):
        for inner in range(4):
            for piece in range(4):
                total = None
                for ref in refs[4 * group : 4 * group + 4]:
                    term = ref[inner, piece].astype(F32)
                    total = term if total is None else total + term
                refs[8 + 4 * group + inner][piece] = total.astype(BF)


def depth_kernel(pos, *refs):
    send, keep, work = refs[8:]
    for group in range(2):
        for weight in range(2):
            for part in range(2):
                total = None
                for ref in refs[4 * group : 4 * group + 4]:
                    term = ref[weight * 2 + part].astype(F32)
                    total = term if total is None else total + term
                work[weight * 4 + group * 2 + part] = total.astype(BF)
    for slot in range(4):
        keep[slot] = work[2 * slot + pos[3] % 2]
        send[slot] = work[2 * slot + 1 - pos[3] % 2]


def add_kernel(one, two, out):
    out[...] = added(one[...], two[...])


def ring_kernel(pos, c0, c2, c4, c6, out, work):
    for index, term in enumerate((c0, c2, c4, c6)):
        work[pos[3] // 2 ^ index] = term[...]
    total = work[0].astype(F32)
    for index in range(1, 4):
        total = total + work[index].astype(F32)
    out[...] = total.astype(BF)


def gather_kernel(*refs):
    for group in range(2):
        for inner in range(4):
            refs[8 + group][inner] = refs[4 * group + inner][...]


def final_kernel(scale, pos, *refs):
    first, second, first_bias, second_bias, rows, ready, sems = refs[8:]
    for group in range(2):
        for outer in range(4):
            for inner in range(4):
                chunk = chunk_of(pos, group, outer, inner)
                for piece in range(4):
                    index = 2 * piece + (pos[3] % 2 ^ group)
                    start = chunk * (4 * PIECE) + (index % 4) * PIECE
                    rows[index // 4, pl.ds(pl.multiple_of(start, 16), PIECE), :] = refs[
                        4 * group + outer
                    ][inner, piece]
    ones = jnp.ones((8, LANES), BF)
    copies = []
    for weight, (target, bias) in enumerate(((first, first_bias), (second, second_bias))):
        for group in range(GROUPS):
            part = slice(group * TAPS // GROUPS, (group + 1) * TAPS // GROUPS)
            for tap in range(part.start, part.stop):
                for side in range(2):
                    start = side * ROWS + tap * HALF
                    ready[weight, tap, :, side * HALF : (side + 1) * HALF] = (
                        rows[weight, start : start + HALF, :].astype(F32) * scale
                    )
            copy = pltpu.make_async_copy(
                ready.at[weight, part], target.at[part], sems.at[weight, group]
            )
            copy.start()
            copies.append(copy)
        sums = lax.dot_general(
            ones,
            rows[weight, TAPS * HALF : ROWS, :],
            (((1,), (1,)), ((), ())),
            preferred_element_type=F32,
        )
        bias[...] = sums[0:1] * scale
    for copy in copies:
        copy.wait()


def exchanged(values, order):
    axes = [axes[order] for axes in GROUP_AXES]
    came = [{0: value[0]} for value in values]
    for mask in MASKS:
        for group in range(2):
            came[group][mask] = across(values[group][mask], axes[group], mask)
    return [value[mask] for value in came for mask in range(4)]


def per_device(features, first_weight, first_bias, second_weight, second_bias, cotangent):
    core = lax.axis_index("chan")
    even = core == 0
    x, y, z = place(lax.axis_index("slab"))
    pos = jnp.stack([core, x, y, z]).astype(jnp.int32)
    first_weight = first_weight.reshape(TAPS, HALF, CH)
    second_weight = second_weight.reshape(TAPS, HALF, CH)
    plane, sums = struct((CH, PLANE)), struct((CH, PLANE), F32)

    feats = features.reshape(CH, PLANE)
    cut = 2 * LANES
    near = to_neighbour(jnp.where(even, feats[:, :cut], feats[:, cut:]))
    far = move(
        jnp.where(even, feats[:, cut:], feats[:, :cut]),
        lambda line: line - 2 if line % 2 else line + 2,
    )
    feats_other = to_sibling(feats)
    first_other = to_sibling(first_weight)
    first_bias, second_bias = first_bias[None], second_bias[None]
    first_bias_other, second_bias_other = to_sibling(first_bias), to_sibling(second_bias)
    partial = conv_call(first_chip_kernel, sums, 4, 2, [pltpu.VMEM((CH, PLANE), BF)], "first_chip")(
        pos, feats, feats_other, first_weight, first_other
    )
    (near, far), partial = tied((near, far), partial)
    first_sum, hidden = conv_call(
        first_kernel, [sums, plane], 7, 1, [pltpu.VMEM((CH, PLANE), BF)], "first"
    )(pos, partial, near, far, first_weight, first_other, first_bias, first_bias_other)

    def chip_part(back, own, sibling, weight, other):
        kernel = functools.partial(chip_kernel, back)
        return conv_call(kernel, sums, 4, 2, [], "chip_back" if back else "chip")(
            pos, own, sibling, weight, other
        )

    second_other = to_sibling(second_weight)
    cots = cotangent.reshape(HALF, 2 * PLANE)
    cots_other = to_sibling(cots)
    near_other, far_other = to_sibling(near), to_sibling(far)
    hidden_sibling, hidden_neighbour = to_sibling(hidden), to_neighbour(hidden)
    partial = chip_part(False, hidden, hidden_sibling, second_weight, second_other)
    hidden_neighbour, partial = tied(hidden_neighbour, partial)
    hidden_near = (hidden, hidden_sibling, hidden_neighbour)
    output, grad_second = conv_call(second_kernel, [plane, plane], 8, 1, [], "second")(
        pos,
        partial,
        hidden_neighbour,
        second_weight,
        second_other,
        second_bias,
        second_bias_other,
        cots,
        cots_other,
    )
    hidden_far = to_sibling(hidden_near[2])

    grad_sibling, grad_neighbour = to_sibling(grad_second), to_neighbour(grad_second)
    second_rows = call(
        term_rows,
        struct((2 * ROWS, LANES)),
        [SMEM] + [VMEM] * 6,
        TERM_SCRATCH,
        CONV_FLOPS,
        5 * 2**20,
        "second_terms",
    )
    second_rows = second_rows(pos, *hidden_near, hidden_far, grad_second, grad_sibling)
    second_rows, grad_sibling = tied(second_rows, grad_sibling)
    partial = chip_part(True, grad_second, grad_sibling, second_weight, second_other)
    output_other = to_sibling(output)
    (grad_neighbour, output_other), partial = tied((grad_neighbour, output_other), partial)
    grad_first = conv_call(hidden_grad_kernel, plane, 5, 1, [], "hidden_grad")(
        pos, partial, grad_neighbour, second_weight, second_other, first_sum
    )

    grad_sibling, grad_neighbour = to_sibling(grad_first), to_neighbour(grad_first)
    quarters = struct((4, 4, PIECE, LANES))
    terms = call(
        first_terms_kernel,
        [quarters] * 8,
        [SMEM] + [VMEM] * 9,
        TERM_SCRATCH + [pltpu.VMEM((2 * ROWS, LANES), BF), pltpu.VMEM((CH, PLANE), BF)],
        CONV_FLOPS,
        9 * 2**20,
        "first_terms",
    )(
        pos, feats, feats_other, near, far, near_other, far_other, grad_first, grad_sibling, second_rows
    )

    terms, grad_neighbour = tied(terms, grad_neighbour)

    came = exchanged((terms[:4], terms[4:]), 0)
    (came[2], came[6]), (grad_here, grad_sibling) = tied((came[2], came[6]), (grad_first, grad_sibling))
    partial = chip_part(True, grad_here, grad_sibling, first_weight, first_other)
    input_grad = conv_call(input_grad_kernel, plane, 4, 1, [], "input_grad")(
        pos, partial, grad_neighbour, first_weight, first_other
    )
    out_placed, grad_placed = call(
        arrange_kernel,
        [struct((HALF, 2 * PLANE)), plane],
        [SMEM] + [VMEM] * 4,
        [],
        2**18,
        2**20,
        "arrange",
    )(pos, output, output_other, input_grad, to_sibling(input_grad))
    out_placed = out_placed.reshape(HALF, 2, 4, LANES)
    grad_placed = grad_placed.reshape(CH, 2, 2, LANES)
    pieces = struct((4, PIECE, LANES))
    spread = call(outer_kernel, [pieces] * 8, [VMEM] * 8, [], 2**21, 5 * 2**20, "outer")(*came)
    groups = exchanged((spread[:4], spread[4:]), 1)
    groups, (out_placed, grad_placed) = tied(groups, (out_placed, grad_placed))
    send, keep = call(
        depth_kernel,
        [pieces] * 2,
        [SMEM] + [VMEM] * 8,
        [pltpu.VMEM((8, PIECE, LANES), BF)],
        2**19,
        2**20,
        "depth",
    )(pos, *groups)
    came = across(send, "z", 1)
    held = call(add_kernel, pieces, [VMEM] * 2, [], 2**17, 2**18, "add")(keep, came)
    held = call(
        ring_kernel,
        pieces,
        [SMEM] + [VMEM] * 4,
        [pltpu.VMEM((4, 4, PIECE, LANES), BF)],
        2**18,
        2**19,
        "ring",
    )(pos, held, *[across(held, "z", mask) for mask in (2, 4, 6)])

    groups = exchanged(([held] * 4, [across(held, "z", 1)] * 4), 1)
    held = call(gather_kernel, [quarters] * 2, [VMEM] * 8, [], 2**18, 4 * 2**20, "gather")(*groups)
    held = exchanged(([held[0]] * 4, [held[1]] * 4), 0)
    scale = 1.0 / math.sqrt(2 * PLANE * lax.axis_size("slab"))
    whole = struct((TAPS, HALF, CH), F32)
    line = struct((1, HALF), F32)
    first_out, second_out, first_bias_out, second_bias_out = call(
        functools.partial(final_kernel, scale),
        [whole, whole, line, line],
        [SMEM] + [VMEM] * 8,
        [
            pltpu.VMEM((2, 2 * ROWS, LANES), BF),
            pltpu.VMEM((2, TAPS, HALF, CH), F32),
            pltpu.SemaphoreType.DMA((2, GROUPS)),
        ],
        2**22,
        12 * 2**20,
        "final",
        out_specs=[ANY, ANY, VMEM, VMEM],
    )(pos, *held)
    shape = (3, 3, 3, HALF, CH)
    return (
        out_placed,
        grad_placed,
        first_out.reshape(shape),
        first_bias_out[0],
        second_out.reshape(shape),
        second_bias_out[0],
    )


def solution(mesh):
    placed = (
        P(None, "slab", "chan", None),
        P(None, None, None, "chan", None),
        P("chan"),
        P(None, None, None, "chan", None),
        P("chan"),
        P("chan", "slab", None, None),
    )
    return jax.shard_map(
        per_device,
        mesh=mesh,
        in_specs=placed,
        out_specs=(
            P("chan", "slab", None, None),
            P(None, "slab", "chan", None),
            P(None, None, None, "chan", None),
            P("chan"),
            P(None, None, None, "chan", None),
            P("chan"),
        ),
        check_vma=False,
    )
```

```python
import functools
import math

import jax
import jax.numpy as jnp
from jax import lax
from jax.experimental import pallas as pl
from jax.experimental.pallas import tpu as pltpu
from jax.sharding import PartitionSpec as P

BF = jnp.bfloat16
F32 = jnp.float32
AXES = ("slab", "chan")
CH = 256
HALF = 128
LANES = 128
PLANE = 512
TAPS = 27
X, Y, Z = 4, 4, 8
DEVICES = 2 * X * Y * Z
ROWS = 28 * HALF
PIECE = 112
GROUPS = 3
GROUP_AXES = (("x", "y"), ("y", "x"))
ORDERS = ((0, 1, 3, 2), (0, 3, 1, 2))
MASKS = (2, 1, 3)
VMEM = pl.BlockSpec(memory_space=pltpu.VMEM)
SMEM = pl.BlockSpec(memory_space=pltpu.SMEM)
ANY = pl.BlockSpec(memory_space=pl.ANY)


def call(kernel, out_shape, in_specs, scratch, flops, moved, name, room=18, out_specs=None):
    return pl.pallas_call(
        kernel,
        out_shape=out_shape,
        in_specs=in_specs,
        out_specs=jax.tree.map(lambda _: VMEM, out_shape) if out_specs is None else out_specs,
        scratch_shapes=scratch,
        compiler_params=pltpu.CompilerParams(vmem_limit_bytes=room * 2**20),
        cost_estimate=pl.CostEstimate(flops=flops, bytes_accessed=moved, transcendentals=0),
        name=name,
    )


def struct(shape, dtype=BF):
    return jax.ShapeDtypeStruct(shape, dtype)


def place(slab):
    return slab % X, (slab // X) % Y, slab // (X * Y)


def slab_of(x, y, z):
    return (z * Y + y) * X + x


def move(value, target):
    pairs = []
    for line in range(DEVICES):
        to = target(line)
        if 0 <= to < DEVICES:
            pairs.append((line, to))
    return lax.ppermute(value, AXES, pairs)


def to_sibling(value):
    return move(value, lambda line: line ^ 1)


def to_neighbour(value):
    return move(value, lambda line: line + 1 if line % 2 else line - 1)


def across(value, axis, mask):
    def target(line):
        x, y, z = place(line // 2)
        if axis == "x":
            x = x ^ mask
        elif axis == "y":
            y = y ^ mask
        else:
            z = z ^ mask
        return slab_of(x, y, z) * 2 + line % 2

    return move(value, target)


def tied(one, two):
    return lax.optimization_barrier((one, two))


def shifted(plane, tap):
    if tap == 1:
        return plane
    wide = plane.astype(F32)
    lane = lax.broadcasted_iota(jnp.int32, (wide.shape[0], LANES), 1)
    parts = []
    for row in range(PLANE // LANES):
        part = wide[:, row * LANES : (row + 1) * LANES]
        if tap == 0:
            part = jnp.where(lane == 0, 0.0, pltpu.roll(part, 1, 1))
        else:
            part = jnp.where(lane == LANES - 1, 0.0, pltpu.roll(part, LANES - 1, 1))
        parts.append(part.astype(BF))
    return jnp.concatenate(parts, axis=1)


def fill(views, index, plane):
    zero = jnp.zeros((CH, LANES), BF)
    for tap in range(3):
        views[tap, index, :, 0:LANES] = zero
        views[tap, index, :, LANES + PLANE :] = zero
        views[tap, index, :, LANES : LANES + PLANE] = shifted(plane, tap)


def half(index, width):
    return pl.ds(pl.multiple_of(index * width, width), width)


def taps():
    return [(x, z, y) for x in range(3) for z in range(3) for y in range(3)]


def own_first(core, plane):
    return jnp.concatenate([plane[half(core, HALF), :], plane[half(1 - core, HALF), :]], axis=0)


def put_halves(core, target, value):
    target[half(core, HALF), :] = value[:HALF]
    target[half(1 - core, HALF), :] = value[HALF:]


def products(weights, views, planes, back):
    total = None
    for index, x in planes:
        for z in range(3):
            for y in range(3):
                tap = x * 9 + z * 3 + y
                if back:
                    tap = TAPS - 1 - tap
                both = jnp.concatenate([weights[0][tap], weights[1][tap]], axis=0)
                term = lax.dot_general(
                    both,
                    views[y, index, :, z * LANES : z * LANES + PLANE],
                    (((0 if back else 1,), (0,)), ((), ())),
                    preferred_element_type=F32,
                )
                total = term if total is None else total + term
    return total


def chip_planes(core):
    return (0, 1), (1, 2 - 2 * core)


def far_plane(core):
    return ((0, 2 * core),)


def sigmoid(value):
    return 1.0 / (1.0 + jnp.exp(-value))


def slope(value):
    sig = sigmoid(value)
    return sig * (1.0 + value * (1.0 - sig))


def bias_column(own, other):
    rows = [jnp.broadcast_to(part[...], (HALF, LANES)).T for part in (own, other)]
    return jnp.concatenate([jnp.concatenate(rows, axis=0)] * (PLANE // LANES), axis=1)


def put_parts(core, plane, mine, theirs):
    plane[:, half(core, 2 * LANES)] = mine
    plane[:, half(1 - core, 2 * LANES)] = theirs


def first_chip_kernel(
    pos, feats, feats_other, w_own, w_other, partial, views, plane
):
    core = pos[0]
    for index, part in enumerate((core, 1 - core)):
        lanes = half(part, 2 * LANES)
        put_parts(core, plane, feats[:, lanes], feats_other[:, lanes])
        fill(views, index, plane[...])
    partial[...] = products((w_own, w_other), views, chip_planes(core), False)


def first_kernel(
    pos, partial, near, far, w_own, w_other, bias, bias_other, sums, hidden, views, plane
):
    core = pos[0]
    put_parts(core, plane, far[...], near[...])
    fill(views, 0, plane[...])
    value = partial[...] + products((w_own, w_other), views, far_plane(core), False) + bias_column(bias, bias_other)
    put_halves(core, sums, value)
    put_halves(core, hidden, (value * sigmoid(value)).astype(BF))


def chip_kernel(back, pos, own, sibling, w_own, w_other, partial, views):
    core = pos[0]
    for index, plane in enumerate((own, sibling)):
        fill(views, index, own_first(core, plane) if back else plane[...])
    partial[...] = products((w_own, w_other), views, chip_planes(core), back)


def second_kernel(
    pos, partial, neighbour, w_own, w_other, bias, bias_other, cots, cots_other, output, grad, views
):
    core = pos[0]
    fill(views, 0, neighbour[...])
    value = partial[...] + products((w_own, w_other), views, far_plane(core), False) + bias_column(bias, bias_other)
    put_halves(core, output, (value * sigmoid(value)).astype(BF))
    lanes = half(core, PLANE)
    cot = jnp.concatenate([cots[:, lanes], cots_other[:, lanes]], axis=0)
    put_halves(core, grad, (cot.astype(F32) * slope(value)).astype(BF))


def hidden_grad_kernel(pos, partial, neighbour, w_own, w_other, sums, grad, views):
    core = pos[0]
    fill(views, 0, own_first(core, neighbour))
    value = partial[...] + products((w_own, w_other), views, far_plane(core), True)
    grad[...] = (value * slope(sums[...])).astype(BF)


def input_grad_kernel(pos, partial, neighbour, w_own, w_other, grad, views):
    core = pos[0]
    fill(views, 0, own_first(core, neighbour))
    value = partial[...] + products((w_own, w_other), views, far_plane(core), True)
    grad[...] = value.astype(BF)


def arrange_kernel(pos, out, out_other, grad, grad_other, out_placed, grad_placed):
    core = pos[0]
    rows, lanes = half(core, HALF), half(core, 2 * LANES)
    out_placed[:, half(core, PLANE)] = out[rows, :]
    out_placed[:, half(1 - core, PLANE)] = out_other[rows, :]
    grad_placed[:, lanes] = grad[:, lanes]
    grad_placed[:, half(1 - core, 2 * LANES)] = grad_other[:, lanes]


CONV_FLOPS = 2 * TAPS * CH * CH * PLANE


def conv_call(kernel, out_shape, operands, planes, scratch, name):
    return call(
        kernel,
        out_shape,
        [SMEM] + [VMEM] * operands,
        [pltpu.VMEM((3, planes, CH, PLANE + 2 * LANES), BF)] + scratch,
        CONV_FLOPS * planes // 3,
        6 * 2**20,
        name,
        room=13,
    )


def chunk_of(pos, group, outer, inner):
    mx, my = (outer, inner) if GROUP_AXES[group][0] == "x" else (inner, outer)
    return (pos[2] ^ my) * X + (pos[1] ^ mx)


def rows_of(pos, group, outer, inner, part):
    start = chunk_of(pos, group, outer, inner) * (4 * PIECE) + (2 * group + part) * PIECE
    return pl.ds(pl.multiple_of(start, 16), PIECE)


def term_rows(pos, own, sibling, neighbour, far, grad_own, grad_sibling, rows, views, grads):
    core = pos[0]
    fill(views, 1 + core, own[...])
    fill(views, 2 - core, sibling[...])
    fill(views, 3 * core, neighbour[...])
    fill(views, 3 - 3 * core, far[...])
    grad_rows(core, grad_own, grad_sibling, rows, views, grads)


def grad_rows(core, grad_own, grad_sibling, rows, views, grads):
    grads[core] = grad_own[half(core, HALF), :]
    grads[1 - core] = grad_sibling[half(core, HALF), :]
    one, two = grads[0], grads[1]
    for x, z, y in taps():
        tap = x * 9 + z * 3 + y
        total = None
        for index, grad in enumerate((one, two)):
            term = lax.dot_general(
                grad,
                views[y, x + index, :, z * LANES : z * LANES + PLANE],
                (((1,), (1,)), ((), ())),
                preferred_element_type=F32,
            )
            total = term if total is None else total + term
        total = total.astype(BF)
        rows[tap * HALF : (tap + 1) * HALF, :] = total[:, :HALF]
        rows[ROWS + tap * HALF : ROWS + (tap + 1) * HALF, :] = total[:, HALF:]
    bias = jnp.zeros((HALF, LANES), F32)
    for grad in (one, two):
        for row in range(PLANE // LANES):
            bias = bias + grad[:, row * LANES : (row + 1) * LANES].astype(F32)
    rows[TAPS * HALF : ROWS, :] = bias.astype(BF)
    rows[ROWS + TAPS * HALF :, :] = jnp.zeros((HALF, LANES), BF)


def first_terms_kernel(
    pos, feats, feats_other, near, far, near_other, far_other, grad_own, grad_sibling, others,
    a0, a1, a2, a3, b0, b1, b2, b3, views, grads, rows, plane
):
    core = pos[0]
    for index, part in ((1 + core, core), (2 - core, 1 - core)):
        lanes = half(part, 2 * LANES)
        put_parts(core, plane, feats[:, lanes], feats_other[:, lanes])
        fill(views, index, plane[...])
    put_parts(core, plane, far[...], near[...])
    fill(views, 3 * core, plane[...])
    put_parts(core, plane, near_other[...], far_other[...])
    fill(views, 3 - 3 * core, plane[...])
    grad_rows(core, grad_own, grad_sibling, rows, views, grads)
    for weight, source in enumerate((rows, others)):
        for group, targets in enumerate(((a0, a1, a2, a3), (b0, b1, b2, b3))):
            for outer in range(4):
                for inner in range(4):
                    for part in range(2):
                        targets[outer][inner, weight * 2 + part] = source[
                            rows_of(pos, group, outer, inner, part), :
                        ]


TERM_SCRATCH = [
    pltpu.VMEM((3, 4, CH, PLANE + 2 * LANES), BF),
    pltpu.VMEM((2, HALF, PLANE), BF),
]


def added(one, two):
    return (one.astype(F32) + two.astype(F32)).astype(BF)


def outer_kernel(*refs):
    for group in range(2):
        for inner in range(4):
            for piece in range(4):
                total = None
                for ref in refs[4 * group : 4 * group + 4]:
                    term = ref[inner, piece].astype(F32)
                    total = term if total is None else total + term
                refs[8 + 4 * group + inner][piece] = total.astype(BF)


def depth_kernel(pos, *refs):
    send, keep, work = refs[8:]
    for group in range(2):
        for weight in range(2):
            for part in range(2):
                total = None
                for ref in refs[4 * group : 4 * group + 4]:
                    term = ref[weight * 2 + part].astype(F32)
                    total = term if total is None else total + term
                work[weight * 4 + group * 2 + part] = total.astype(BF)
    for slot in range(4):
        keep[slot] = work[2 * slot + pos[3] % 2]
        send[slot] = work[2 * slot + 1 - pos[3] % 2]


def add_kernel(one, two, out):
    out[...] = added(one[...], two[...])


def ring_kernel(pos, c0, c2, c4, c6, out, work):
    for index, term in enumerate((c0, c2, c4, c6)):
        work[pos[3] // 2 ^ index] = term[...]
    total = work[0].astype(F32)
    for index in range(1, 4):
        total = total + work[index].astype(F32)
    out[...] = total.astype(BF)


def gather_kernel(*refs):
    for group in range(2):
        for inner in range(4):
            for part in range(2):
                refs[8 + group * 2 + part][inner] = refs[4 * group + inner][2 * part : 2 * part + 2]


def join_kernel(*refs):
    for stream in range(4):
        refs[8 + stream][0:4] = refs[stream][...]
        refs[8 + stream][4:8] = refs[4 + stream][...]


def final_kernel(scale, pos, *refs):
    first, second, first_bias, second_bias, rows, ready, sems = refs[8:]
    for stream in range(4):
        group, half_of = stream // 2, stream % 2
        for slot, outer in enumerate(ORDERS[half_of]):
            source = refs[stream] if slot < 2 else refs[4 + stream]
            for inner in range(4):
                chunk = chunk_of(pos, group, outer, inner)
                for part in range(2):
                    index = 2 * (2 * half_of + part) + (pos[3] % 2 ^ group)
                    start = chunk * (4 * PIECE) + (index % 4) * PIECE
                    rows[index // 4, pl.ds(pl.multiple_of(start, 16), PIECE), :] = source[
                        (slot % 2) * 4 + inner, part
                    ]
    ones = jnp.ones((8, LANES), BF)
    copies = []
    for weight, (target, bias) in enumerate(((first, first_bias), (second, second_bias))):
        for group in range(GROUPS):
            part = slice(group * TAPS // GROUPS, (group + 1) * TAPS // GROUPS)
            for tap in range(part.start, part.stop):
                for side in range(2):
                    start = side * ROWS + tap * HALF
                    ready[weight, tap, :, side * HALF : (side + 1) * HALF] = (
                        rows[weight, start : start + HALF, :].astype(F32) * scale
                    )
            copy = pltpu.make_async_copy(
                ready.at[weight, part], target.at[part], sems.at[weight, group]
            )
            copy.start()
            copies.append(copy)
        sums = lax.dot_general(
            ones,
            rows[weight, TAPS * HALF : ROWS, :],
            (((1,), (1,)), ((), ())),
            preferred_element_type=F32,
        )
        bias[...] = sums[0:1] * scale
    for copy in copies:
        copy.wait()


def exchanged(values, order):
    axes = [axes[order] for axes in GROUP_AXES]
    came = [{0: value[0]} for value in values]
    for mask in MASKS:
        for group in range(2):
            came[group][mask] = across(values[group][mask], axes[group], mask)
    return [value[mask] for value in came for mask in range(4)]


def swapped(values, order):
    return [
        across(value, GROUP_AXES[stream // 2][0], ORDERS[stream % 2][order])
        for stream, value in enumerate(values)
    ]


def per_device(features, first_weight, first_bias, second_weight, second_bias, cotangent):
    core = lax.axis_index("chan")
    even = core == 0
    x, y, z = place(lax.axis_index("slab"))
    pos = jnp.stack([core, x, y, z]).astype(jnp.int32)
    first_weight = first_weight.reshape(TAPS, HALF, CH)
    second_weight = second_weight.reshape(TAPS, HALF, CH)
    plane, sums = struct((CH, PLANE)), struct((CH, PLANE), F32)

    feats = features.reshape(CH, PLANE)
    cots = cotangent.reshape(HALF, 2 * PLANE)
    feats, cots = tied(feats, cots)
    cut = 2 * LANES
    near = to_neighbour(jnp.where(even, feats[:, :cut], feats[:, cut:]))
    far = move(
        jnp.where(even, feats[:, cut:], feats[:, :cut]),
        lambda line: line - 2 if line % 2 else line + 2,
    )
    feats_other = to_sibling(feats)
    first_other = to_sibling(first_weight)
    first_bias, second_bias = first_bias[None], second_bias[None]
    first_bias_other, second_bias_other = to_sibling(first_bias), to_sibling(second_bias)
    partial = conv_call(first_chip_kernel, sums, 4, 2, [pltpu.VMEM((CH, PLANE), BF)], "first_chip")(
        pos, feats, feats_other, first_weight, first_other
    )
    (near, far), partial = tied((near, far), partial)
    first_sum, hidden = conv_call(
        first_kernel, [sums, plane], 7, 1, [pltpu.VMEM((CH, PLANE), BF)], "first"
    )(pos, partial, near, far, first_weight, first_other, first_bias, first_bias_other)

    def chip_part(back, own, sibling, weight, other):
        kernel = functools.partial(chip_kernel, back)
        return conv_call(kernel, sums, 4, 2, [], "chip_back" if back else "chip")(
            pos, own, sibling, weight, other
        )

    second_other = to_sibling(second_weight)
    cots_other = to_sibling(cots)
    near_other, far_other = to_sibling(near), to_sibling(far)
    hidden_sibling, hidden_neighbour = to_sibling(hidden), to_neighbour(hidden)
    partial = chip_part(False, hidden, hidden_sibling, second_weight, second_other)
    hidden_neighbour, partial = tied(hidden_neighbour, partial)
    hidden_near = (hidden, hidden_sibling, hidden_neighbour)
    output, grad_second = conv_call(second_kernel, [plane, plane], 8, 1, [], "second")(
        pos,
        partial,
        hidden_neighbour,
        second_weight,
        second_other,
        second_bias,
        second_bias_other,
        cots,
        cots_other,
    )
    hidden_far = to_sibling(hidden_near[2])

    grad_sibling, grad_neighbour = to_sibling(grad_second), to_neighbour(grad_second)
    second_rows = call(
        term_rows,
        struct((2 * ROWS, LANES)),
        [SMEM] + [VMEM] * 6,
        TERM_SCRATCH,
        CONV_FLOPS,
        5 * 2**20,
        "second_terms",
    )
    second_rows = second_rows(pos, *hidden_near, hidden_far, grad_second, grad_sibling)
    second_rows, grad_sibling = tied(second_rows, grad_sibling)
    partial = chip_part(True, grad_second, grad_sibling, second_weight, second_other)
    output_other = to_sibling(output)
    (grad_neighbour, output_other), partial = tied((grad_neighbour, output_other), partial)
    grad_first = conv_call(hidden_grad_kernel, plane, 5, 1, [], "hidden_grad")(
        pos, partial, grad_neighbour, second_weight, second_other, first_sum
    )

    grad_sibling, grad_neighbour = to_sibling(grad_first), to_neighbour(grad_first)
    quarters = struct((4, 4, PIECE, LANES))
    terms = call(
        first_terms_kernel,
        [quarters] * 8,
        [SMEM] + [VMEM] * 9,
        TERM_SCRATCH + [pltpu.VMEM((2 * ROWS, LANES), BF), pltpu.VMEM((CH, PLANE), BF)],
        CONV_FLOPS,
        9 * 2**20,
        "first_terms",
    )(
        pos, feats, feats_other, near, far, near_other, far_other, grad_first, grad_sibling, second_rows
    )

    terms, grad_neighbour = tied(terms, grad_neighbour)

    came = exchanged((terms[:4], terms[4:]), 0)
    (came[2], came[6]), (grad_here, grad_sibling) = tied((came[2], came[6]), (grad_first, grad_sibling))
    partial = chip_part(True, grad_here, grad_sibling, first_weight, first_other)
    input_grad = conv_call(input_grad_kernel, plane, 4, 1, [], "input_grad")(
        pos, partial, grad_neighbour, first_weight, first_other
    )
    out_placed, grad_placed = call(
        arrange_kernel,
        [struct((HALF, 2 * PLANE)), plane],
        [SMEM] + [VMEM] * 4,
        [],
        2**18,
        2**20,
        "arrange",
    )(pos, output, output_other, input_grad, to_sibling(input_grad))
    out_placed, grad_placed = out_placed.reshape(HALF, 2, 4, LANES), grad_placed.reshape(CH, 2, 2, LANES)
    pieces = struct((4, PIECE, LANES))
    spread = call(outer_kernel, [pieces] * 8, [VMEM] * 8, [], 2**21, 5 * 2**20, "outer")(*came)
    groups = exchanged((spread[:4], spread[4:]), 1)
    groups, (out_placed, grad_placed) = tied(groups, (out_placed, grad_placed))
    send, keep = call(
        depth_kernel,
        [pieces] * 2,
        [SMEM] + [VMEM] * 8,
        [pltpu.VMEM((8, PIECE, LANES), BF)],
        2**19,
        2**20,
        "depth",
    )(pos, *groups)
    came = across(send, "z", 1)
    held = call(add_kernel, pieces, [VMEM] * 2, [], 2**17, 2**18, "add")(keep, came)
    held = call(
        ring_kernel,
        pieces,
        [SMEM] + [VMEM] * 4,
        [pltpu.VMEM((4, 4, PIECE, LANES), BF)],
        2**18,
        2**19,
        "ring",
    )(pos, held, *[across(held, "z", mask) for mask in (2, 4, 6)])

    groups = exchanged(([held] * 4, [across(held, "z", 1)] * 4), 1)
    half_size, full_size = struct((4, 2, PIECE, LANES)), struct((8, 2, PIECE, LANES))
    held = call(gather_kernel, [half_size] * 4, [VMEM] * 8, [], 2**18, 4 * 2**20, "gather")(*groups)
    came = swapped(held, 1)
    held = call(join_kernel, [full_size] * 4, [VMEM] * 8, [], 2**18, 4 * 2**20, "join")(*held, *came)
    came = swapped(held, 2)
    scale = 1.0 / math.sqrt(2 * PLANE * lax.axis_size("slab"))
    whole = struct((TAPS, HALF, CH), F32)
    line = struct((1, HALF), F32)
    first_out, second_out, first_bias_out, second_bias_out = call(
        functools.partial(final_kernel, scale),
        [whole, whole, line, line],
        [SMEM] + [VMEM] * 8,
        [
            pltpu.VMEM((2, 2 * ROWS, LANES), BF),
            pltpu.VMEM((2, TAPS, HALF, CH), F32),
            pltpu.SemaphoreType.DMA((2, GROUPS)),
        ],
        2**22,
        12 * 2**20,
        "final",
        out_specs=[ANY, ANY, VMEM, VMEM],
    )(pos, *held, *came)
    shape = (3, 3, 3, HALF, CH)
    return (
        out_placed,
        grad_placed,
        first_out.reshape(shape),
        first_bias_out[0],
        second_out.reshape(shape),
        second_bias_out[0],
    )


def solution(mesh):
    placed = (
        P(None, "slab", "chan", None),
        P(None, None, None, "chan", None),
        P("chan"),
        P(None, None, None, "chan", None),
        P("chan"),
        P("chan", "slab", None, None),
    )
    return jax.shard_map(
        per_device,
        mesh=mesh,
        in_specs=placed,
        out_specs=(
            P("chan", "slab", None, None),
            P(None, "slab", "chan", None),
            P(None, None, None, "chan", None),
            P("chan"),
            P(None, None, None, "chan", None),
            P("chan"),
        ),
        check_vma=False,
    )
```

```python
import functools
import math

import jax
import jax.numpy as jnp
from jax import lax
from jax.experimental import pallas as pl
from jax.experimental.pallas import tpu as pltpu
from jax.sharding import PartitionSpec as P

BF = jnp.bfloat16
F32 = jnp.float32
AXES = ("slab", "chan")
CH = 256
HALF = 128
LANES = 128
PLANE = 512
TAPS = 27
X, Y, Z = 4, 4, 8
DEVICES = 2 * X * Y * Z
ROWS = 28 * HALF
PIECE = 112
GROUPS = 3
GROUP_AXES = (("x", "y"), ("y", "x"))
ORDERS = ((0, 1, 3, 2), (0, 3, 1, 2))
MASKS = (2, 1, 3)
VMEM = pl.BlockSpec(memory_space=pltpu.VMEM)
SMEM = pl.BlockSpec(memory_space=pltpu.SMEM)
ANY = pl.BlockSpec(memory_space=pl.ANY)


def call(kernel, out_shape, in_specs, scratch, flops, moved, name, room=18, out_specs=None):
    return pl.pallas_call(
        kernel,
        out_shape=out_shape,
        in_specs=in_specs,
        out_specs=jax.tree.map(lambda _: VMEM, out_shape) if out_specs is None else out_specs,
        scratch_shapes=scratch,
        compiler_params=pltpu.CompilerParams(vmem_limit_bytes=room * 2**20),
        cost_estimate=pl.CostEstimate(flops=flops, bytes_accessed=moved, transcendentals=0),
        name=name,
    )


def struct(shape, dtype=BF):
    return jax.ShapeDtypeStruct(shape, dtype)


def place(slab):
    return slab % X, (slab // X) % Y, slab // (X * Y)


def slab_of(x, y, z):
    return (z * Y + y) * X + x


def move(value, target):
    pairs = []
    for line in range(DEVICES):
        to = target(line)
        if 0 <= to < DEVICES:
            pairs.append((line, to))
    return lax.ppermute(value, AXES, pairs)


def to_sibling(value):
    return move(value, lambda line: line ^ 1)


def to_neighbour(value):
    return move(value, lambda line: line + 1 if line % 2 else line - 1)


def across(value, axis, mask):
    def target(line):
        x, y, z = place(line // 2)
        if axis == "x":
            x = x ^ mask
        elif axis == "y":
            y = y ^ mask
        else:
            z = z ^ mask
        return slab_of(x, y, z) * 2 + line % 2

    return move(value, target)


def tied(one, two):
    return lax.optimization_barrier((one, two))


def shifted(plane, tap):
    if tap == 1:
        return plane
    wide = plane.astype(F32)
    lane = lax.broadcasted_iota(jnp.int32, (wide.shape[0], LANES), 1)
    parts = []
    for row in range(PLANE // LANES):
        part = wide[:, row * LANES : (row + 1) * LANES]
        if tap == 0:
            part = jnp.where(lane == 0, 0.0, pltpu.roll(part, 1, 1))
        else:
            part = jnp.where(lane == LANES - 1, 0.0, pltpu.roll(part, LANES - 1, 1))
        parts.append(part.astype(BF))
    return jnp.concatenate(parts, axis=1)


def fill(views, index, plane):
    zero = jnp.zeros((CH, LANES), BF)
    for tap in range(3):
        views[tap, index, :, 0:LANES] = zero
        views[tap, index, :, LANES + PLANE :] = zero
        views[tap, index, :, LANES : LANES + PLANE] = shifted(plane, tap)


def half(index, width):
    return pl.ds(pl.multiple_of(index * width, width), width)


def taps():
    return [(x, z, y) for x in range(3) for z in range(3) for y in range(3)]


def own_first(core, plane):
    return jnp.concatenate([plane[half(core, HALF), :], plane[half(1 - core, HALF), :]], axis=0)


def put_halves(core, target, value):
    target[half(core, HALF), :] = value[:HALF]
    target[half(1 - core, HALF), :] = value[HALF:]


def products(weights, views, planes, back):
    total = None
    for index, x in planes:
        for z in range(3):
            for y in range(3):
                tap = x * 9 + z * 3 + y
                if back:
                    tap = TAPS - 1 - tap
                both = jnp.concatenate([weights[0][tap], weights[1][tap]], axis=0)
                term = lax.dot_general(
                    both,
                    views[y, index, :, z * LANES : z * LANES + PLANE],
                    (((0 if back else 1,), (0,)), ((), ())),
                    preferred_element_type=F32,
                )
                total = term if total is None else total + term
    return total


def chip_planes(core):
    return (0, 1), (1, 2 - 2 * core)


def far_plane(core):
    return ((0, 2 * core),)


def sigmoid(value):
    return 1.0 / (1.0 + jnp.exp(-value))


def slope(value):
    sig = sigmoid(value)
    return sig * (1.0 + value * (1.0 - sig))


def bias_column(own, other):
    rows = [jnp.broadcast_to(part[...], (HALF, LANES)).T for part in (own, other)]
    return jnp.concatenate([jnp.concatenate(rows, axis=0)] * (PLANE // LANES), axis=1)


def put_parts(core, plane, mine, theirs):
    plane[:, half(core, 2 * LANES)] = mine
    plane[:, half(1 - core, 2 * LANES)] = theirs


def first_chip_kernel(
    pos, feats, feats_other, w_own, w_other, partial, views, plane
):
    core = pos[0]
    for index, part in enumerate((core, 1 - core)):
        lanes = half(part, 2 * LANES)
        put_parts(core, plane, feats[:, lanes], feats_other[:, lanes])
        fill(views, index, plane[...])
    partial[...] = products((w_own, w_other), views, chip_planes(core), False)


def first_kernel(
    pos, partial, near, far, w_own, w_other, bias, bias_other, sums, hidden, views, plane
):
    core = pos[0]
    put_parts(core, plane, far[...], near[...])
    fill(views, 0, plane[...])
    value = partial[...] + products((w_own, w_other), views, far_plane(core), False) + bias_column(bias, bias_other)
    put_halves(core, sums, value)
    put_halves(core, hidden, (value * sigmoid(value)).astype(BF))


def chip_kernel(back, pos, own, sibling, w_own, w_other, partial, views):
    core = pos[0]
    for index, plane in enumerate((own, sibling)):
        fill(views, index, own_first(core, plane) if back else plane[...])
    partial[...] = products((w_own, w_other), views, chip_planes(core), back)


def unrolled(core, cots):
    return jnp.concatenate([cots[:, core, row, :] for row in range(PLANE // LANES)], axis=1)


def cot_kernel(pos, cots, cots_other, cot):
    cot[:HALF, :] = unrolled(pos[0], cots)
    cot[HALF:, :] = unrolled(pos[0], cots_other)


def second_kernel(
    pos, partial, neighbour, w_own, w_other, bias, bias_other, cot, output, grad, views
):
    core = pos[0]
    fill(views, 0, neighbour[...])
    value = partial[...] + products((w_own, w_other), views, far_plane(core), False) + bias_column(bias, bias_other)
    put_halves(core, output, (value * sigmoid(value)).astype(BF))
    put_halves(core, grad, (cot[...].astype(F32) * slope(value)).astype(BF))


def hidden_grad_kernel(pos, partial, neighbour, w_own, w_other, sums, grad, views):
    core = pos[0]
    fill(views, 0, own_first(core, neighbour))
    value = partial[...] + products((w_own, w_other), views, far_plane(core), True)
    grad[...] = (value * slope(sums[...])).astype(BF)


def input_grad_kernel(pos, partial, neighbour, w_own, w_other, grad, views):
    core = pos[0]
    fill(views, 0, own_first(core, neighbour))
    value = partial[...] + products((w_own, w_other), views, far_plane(core), True)
    grad[...] = value.astype(BF)


def arrange_kernel(pos, out, out_other, grad, grad_other, out_placed, grad_placed):
    core = pos[0]
    rows, lanes = half(core, HALF), half(core, 2 * LANES)
    out_placed[:, half(core, PLANE)] = out[rows, :]
    out_placed[:, half(1 - core, PLANE)] = out_other[rows, :]
    grad_placed[:, lanes] = grad[:, lanes]
    grad_placed[:, half(1 - core, 2 * LANES)] = grad_other[:, lanes]


CONV_FLOPS = 2 * TAPS * CH * CH * PLANE


def conv_call(kernel, out_shape, operands, planes, scratch, name):
    return call(
        kernel,
        out_shape,
        [SMEM] + [VMEM] * operands,
        [pltpu.VMEM((3, planes, CH, PLANE + 2 * LANES), BF)] + scratch,
        CONV_FLOPS * planes // 3,
        6 * 2**20,
        name,
        room=13,
    )


def chunk_of(pos, group, outer, inner):
    mx, my = (outer, inner) if GROUP_AXES[group][0] == "x" else (inner, outer)
    return (pos[2] ^ my) * X + (pos[1] ^ mx)


def rows_of(pos, group, outer, inner, part):
    start = chunk_of(pos, group, outer, inner) * (4 * PIECE) + (2 * group + part) * PIECE
    return pl.ds(pl.multiple_of(start, 16), PIECE)


def term_rows(pos, own, sibling, neighbour, far, grad_own, grad_sibling, rows, views, grads):
    core = pos[0]
    fill(views, 1 + core, own[...])
    fill(views, 2 - core, sibling[...])
    fill(views, 3 * core, neighbour[...])
    fill(views, 3 - 3 * core, far[...])
    grad_rows(core, grad_own, grad_sibling, rows, views, grads)


def grad_rows(core, grad_own, grad_sibling, rows, views, grads):
    grads[core] = grad_own[half(core, HALF), :]
    grads[1 - core] = grad_sibling[half(core, HALF), :]
    one, two = grads[0], grads[1]
    for x, z, y in taps():
        tap = x * 9 + z * 3 + y
        total = None
        for index, grad in enumerate((one, two)):
            term = lax.dot_general(
                grad,
                views[y, x + index, :, z * LANES : z * LANES + PLANE],
                (((1,), (1,)), ((), ())),
                preferred_element_type=F32,
            )
            total = term if total is None else total + term
        total = total.astype(BF)
        rows[tap * HALF : (tap + 1) * HALF, :] = total[:, :HALF]
        rows[ROWS + tap * HALF : ROWS + (tap + 1) * HALF, :] = total[:, HALF:]
    bias = jnp.zeros((HALF, LANES), F32)
    for grad in (one, two):
        for row in range(PLANE // LANES):
            bias = bias + grad[:, row * LANES : (row + 1) * LANES].astype(F32)
    rows[TAPS * HALF : ROWS, :] = bias.astype(BF)
    rows[ROWS + TAPS * HALF :, :] = jnp.zeros((HALF, LANES), BF)


def first_terms_kernel(
    pos, feats, feats_other, near, far, near_other, far_other, grad_own, grad_sibling, others,
    a0, a1, a2, a3, b0, b1, b2, b3, views, grads, rows, plane
):
    core = pos[0]
    for index, part in ((1 + core, core), (2 - core, 1 - core)):
        lanes = half(part, 2 * LANES)
        put_parts(core, plane, feats[:, lanes], feats_other[:, lanes])
        fill(views, index, plane[...])
    put_parts(core, plane, far[...], near[...])
    fill(views, 3 * core, plane[...])
    put_parts(core, plane, near_other[...], far_other[...])
    fill(views, 3 - 3 * core, plane[...])
    grad_rows(core, grad_own, grad_sibling, rows, views, grads)
    for weight, source in enumerate((rows, others)):
        for group, targets in enumerate(((a0, a1, a2, a3), (b0, b1, b2, b3))):
            for outer in range(4):
                for inner in range(4):
                    for part in range(2):
                        targets[outer][inner, weight * 2 + part] = source[
                            rows_of(pos, group, outer, inner, part), :
                        ]


TERM_SCRATCH = [
    pltpu.VMEM((3, 4, CH, PLANE + 2 * LANES), BF),
    pltpu.VMEM((2, HALF, PLANE), BF),
]


def added(one, two):
    return (one.astype(F32) + two.astype(F32)).astype(BF)


def outer_kernel(*refs):
    for group in range(2):
        for inner in range(4):
            for piece in range(4):
                total = None
                for ref in refs[4 * group : 4 * group + 4]:
                    term = ref[inner, piece].astype(F32)
                    total = term if total is None else total + term
                refs[8 + 4 * group + inner][piece] = total.astype(BF)


def depth_kernel(pos, *refs):
    send, keep, work = refs[8:]
    for group in range(2):
        for weight in range(2):
            for part in range(2):
                total = None
                for ref in refs[4 * group : 4 * group + 4]:
                    term = ref[weight * 2 + part].astype(F32)
                    total = term if total is None else total + term
                work[weight * 4 + group * 2 + part] = total.astype(BF)
    for slot in range(4):
        keep[slot] = work[2 * slot + pos[3] % 2]
        send[slot] = work[2 * slot + 1 - pos[3] % 2]


def add_kernel(one, two, out):
    out[...] = added(one[...], two[...])


def ring_kernel(pos, c0, c2, c4, c6, out, work):
    for index, term in enumerate((c0, c2, c4, c6)):
        work[pos[3] // 2 ^ index] = term[...]
    total = work[0].astype(F32)
    for index in range(1, 4):
        total = total + work[index].astype(F32)
    out[...] = total.astype(BF)


def gather_kernel(*refs):
    for group in range(2):
        for inner in range(4):
            for part in range(2):
                refs[8 + group * 2 + part][inner] = refs[4 * group + inner][2 * part : 2 * part + 2]


def join_kernel(*refs):
    for stream in range(4):
        refs[8 + stream][0:4] = refs[stream][...]
        refs[8 + stream][4:8] = refs[4 + stream][...]


def final_kernel(scale, pos, *refs):
    first, second, first_bias, second_bias, rows, ready, sems = refs[8:]
    for stream in range(4):
        group, half_of = stream // 2, stream % 2
        for slot, outer in enumerate(ORDERS[half_of]):
            source = refs[stream] if slot < 2 else refs[4 + stream]
            for inner in range(4):
                chunk = chunk_of(pos, group, outer, inner)
                for part in range(2):
                    index = 2 * (2 * half_of + part) + (pos[3] % 2 ^ group)
                    start = chunk * (4 * PIECE) + (index % 4) * PIECE
                    rows[index // 4, pl.ds(pl.multiple_of(start, 16), PIECE), :] = source[
                        (slot % 2) * 4 + inner, part
                    ]
    ones = jnp.ones((8, LANES), BF)
    copies = []
    for weight, (target, bias) in enumerate(((first, first_bias), (second, second_bias))):
        for group in range(GROUPS):
            part = slice(group * TAPS // GROUPS, (group + 1) * TAPS // GROUPS)
            for tap in range(part.start, part.stop):
                for side in range(2):
                    start = side * ROWS + tap * HALF
                    ready[weight, tap, :, side * HALF : (side + 1) * HALF] = (
                        rows[weight, start : start + HALF, :].astype(F32) * scale
                    )
            copy = pltpu.make_async_copy(
                ready.at[weight, part], target.at[part], sems.at[weight, group]
            )
            copy.start()
            copies.append(copy)
        sums = lax.dot_general(
            ones,
            rows[weight, TAPS * HALF : ROWS, :],
            (((1,), (1,)), ((), ())),
            preferred_element_type=F32,
        )
        bias[...] = sums[0:1] * scale
    for copy in copies:
        copy.wait()


def exchanged(values, order):
    axes = [axes[order] for axes in GROUP_AXES]
    came = [{0: value[0]} for value in values]
    for mask in MASKS:
        for group in range(2):
            came[group][mask] = across(values[group][mask], axes[group], mask)
    return [value[mask] for value in came for mask in range(4)]


def swapped(values, order):
    return [
        across(value, GROUP_AXES[stream // 2][0], ORDERS[stream % 2][order])
        for stream, value in enumerate(values)
    ]


def per_device(features, first_weight, first_bias, second_weight, second_bias, cotangent):
    core = lax.axis_index("chan")
    even = core == 0
    x, y, z = place(lax.axis_index("slab"))
    pos = jnp.stack([core, x, y, z]).astype(jnp.int32)
    first_weight = first_weight.reshape(TAPS, HALF, CH)
    second_weight = second_weight.reshape(TAPS, HALF, CH)
    plane, sums = struct((CH, PLANE)), struct((CH, PLANE), F32)

    feats = features.reshape(CH, PLANE)
    cut = 2 * LANES
    near = to_neighbour(jnp.where(even, feats[:, :cut], feats[:, cut:]))
    far = move(
        jnp.where(even, feats[:, cut:], feats[:, :cut]),
        lambda line: line - 2 if line % 2 else line + 2,
    )
    feats_other = to_sibling(feats)
    first_other = to_sibling(first_weight)
    first_bias, second_bias = first_bias[None], second_bias[None]
    first_bias_other, second_bias_other = to_sibling(first_bias), to_sibling(second_bias)
    partial = conv_call(first_chip_kernel, sums, 4, 2, [pltpu.VMEM((CH, PLANE), BF)], "first_chip")(
        pos, feats, feats_other, first_weight, first_other
    )
    (near, far), partial = tied((near, far), partial)
    first_sum, hidden = conv_call(
        first_kernel, [sums, plane], 7, 1, [pltpu.VMEM((CH, PLANE), BF)], "first"
    )(pos, partial, near, far, first_weight, first_other, first_bias, first_bias_other)

    def chip_part(back, own, sibling, weight, other):
        kernel = functools.partial(chip_kernel, back)
        return conv_call(kernel, sums, 4, 2, [], "chip_back" if back else "chip")(
            pos, own, sibling, weight, other
        )

    second_other = to_sibling(second_weight)
    cots_other = to_sibling(cotangent)
    near_other, far_other = to_sibling(near), to_sibling(far)
    hidden_sibling, hidden_neighbour = to_sibling(hidden), to_neighbour(hidden)
    partial = chip_part(False, hidden, hidden_sibling, second_weight, second_other)
    cot = call(cot_kernel, plane, [SMEM, VMEM, VMEM], [], 2**18, 2**20, "cot")(
        pos, cotangent, cots_other
    )
    hidden_neighbour, (partial, cot) = tied(hidden_neighbour, (partial, cot))
    hidden_near = (hidden, hidden_sibling, hidden_neighbour)
    output, grad_second = conv_call(second_kernel, [plane, plane], 7, 1, [], "second")(
        pos,
        partial,
        hidden_neighbour,
        second_weight,
        second_other,
        second_bias,
        second_bias_other,
        cot,
    )
    hidden_far = to_sibling(hidden_near[2])

    grad_sibling, grad_neighbour = to_sibling(grad_second), to_neighbour(grad_second)
    second_rows = call(
        term_rows,
        struct((2 * ROWS, LANES)),
        [SMEM] + [VMEM] * 6,
        TERM_SCRATCH,
        CONV_FLOPS,
        5 * 2**20,
        "second_terms",
    )
    second_rows = second_rows(pos, *hidden_near, hidden_far, grad_second, grad_sibling)
    second_rows, grad_sibling = tied(second_rows, grad_sibling)
    partial = chip_part(True, grad_second, grad_sibling, second_weight, second_other)
    output_other = to_sibling(output)
    (grad_neighbour, output_other), partial = tied((grad_neighbour, output_other), partial)
    grad_first = conv_call(hidden_grad_kernel, plane, 5, 1, [], "hidden_grad")(
        pos, partial, grad_neighbour, second_weight, second_other, first_sum
    )

    grad_sibling, grad_neighbour = to_sibling(grad_first), to_neighbour(grad_first)
    quarters = struct((4, 4, PIECE, LANES))
    terms = call(
        first_terms_kernel,
        [quarters] * 8,
        [SMEM] + [VMEM] * 9,
        TERM_SCRATCH + [pltpu.VMEM((2 * ROWS, LANES), BF), pltpu.VMEM((CH, PLANE), BF)],
        CONV_FLOPS,
        9 * 2**20,
        "first_terms",
    )(
        pos, feats, feats_other, near, far, near_other, far_other, grad_first, grad_sibling, second_rows
    )

    terms, grad_neighbour = tied(terms, grad_neighbour)

    came = exchanged((terms[:4], terms[4:]), 0)
    (came[2], came[6]), (grad_here, grad_sibling) = tied((came[2], came[6]), (grad_first, grad_sibling))
    partial = chip_part(True, grad_here, grad_sibling, first_weight, first_other)
    input_grad = conv_call(input_grad_kernel, plane, 4, 1, [], "input_grad")(
        pos, partial, grad_neighbour, first_weight, first_other
    )
    pieces = struct((4, PIECE, LANES))
    spread = call(outer_kernel, [pieces] * 8, [VMEM] * 8, [], 2**21, 5 * 2**20, "outer")(*came)
    groups = exchanged((spread[:4], spread[4:]), 1)
    send, keep = call(
        depth_kernel,
        [pieces] * 2,
        [SMEM] + [VMEM] * 8,
        [pltpu.VMEM((8, PIECE, LANES), BF)],
        2**19,
        2**20,
        "depth",
    )(pos, *groups)
    came = across(send, "z", 1)
    held = call(add_kernel, pieces, [VMEM] * 2, [], 2**17, 2**18, "add")(keep, came)
    held, input_grad = tied(held, input_grad)
    came = [across(held, "z", mask) for mask in (2, 4, 6)]
    out_placed, grad_placed = call(
        arrange_kernel,
        [struct((HALF, 2 * PLANE)), plane],
        [SMEM] + [VMEM] * 4,
        [],
        2**18,
        2**20,
        "arrange",
    )(pos, output, output_other, input_grad, to_sibling(input_grad))
    out_placed, grad_placed = out_placed.reshape(HALF, 2, 4, LANES), grad_placed.reshape(CH, 2, 2, LANES)
    came, (out_placed, grad_placed) = tied(came, (out_placed, grad_placed))
    held = call(
        ring_kernel,
        pieces,
        [SMEM] + [VMEM] * 4,
        [pltpu.VMEM((4, 4, PIECE, LANES), BF)],
        2**18,
        2**19,
        "ring",
    )(pos, held, *came)

    groups = exchanged(([held] * 4, [across(held, "z", 1)] * 4), 1)
    half_size, full_size = struct((4, 2, PIECE, LANES)), struct((8, 2, PIECE, LANES))
    held = call(gather_kernel, [half_size] * 4, [VMEM] * 8, [], 2**18, 4 * 2**20, "gather")(*groups)
    came = swapped(held, 1)
    held = call(join_kernel, [full_size] * 4, [VMEM] * 8, [], 2**18, 4 * 2**20, "join")(*held, *came)
    came = swapped(held, 2)
    scale = 1.0 / math.sqrt(2 * PLANE * lax.axis_size("slab"))
    whole = struct((TAPS, HALF, CH), F32)
    line = struct((1, HALF), F32)
    first_out, second_out, first_bias_out, second_bias_out = call(
        functools.partial(final_kernel, scale),
        [whole, whole, line, line],
        [SMEM] + [VMEM] * 8,
        [
            pltpu.VMEM((2, 2 * ROWS, LANES), BF),
            pltpu.VMEM((2, TAPS, HALF, CH), F32),
            pltpu.SemaphoreType.DMA((2, GROUPS)),
        ],
        2**22,
        12 * 2**20,
        "final",
        out_specs=[ANY, ANY, VMEM, VMEM],
    )(pos, *held, *came)
    shape = (3, 3, 3, HALF, CH)
    return (
        out_placed,
        grad_placed,
        first_out.reshape(shape),
        first_bias_out[0],
        second_out.reshape(shape),
        second_bias_out[0],
    )


def solution(mesh):
    placed = (
        P(None, "slab", "chan", None),
        P(None, None, None, "chan", None),
        P("chan"),
        P(None, None, None, "chan", None),
        P("chan"),
        P("chan", "slab", None, None),
    )
    return jax.shard_map(
        per_device,
        mesh=mesh,
        in_specs=placed,
        out_specs=(
            P("chan", "slab", None, None),
            P(None, "slab", "chan", None),
            P(None, None, None, "chan", None),
            P("chan"),
            P(None, None, None, "chan", None),
            P("chan"),
        ),
        check_vma=False,
    )
```
